32 devices in a mesh: tile: 4 (over x, core), orient: 8 (over z, y).
Axes of the slice: x: 2, y: 2, z: 4, core: 2. Of those that a mesh axis runs over, the one named last changes fastest.
Arguments:
- micrograph: float32 [2048, 512], P('tile'), may hold values from -40 to 40
- templates: float32 [8, 256, 256], P('orient', 'tile'), may hold values from -6 to 6
- defocus_values: float32 [4], replicated, may hold values from 5000 to 20000
- defocus_group: int32 [4], P('tile'), may hold values from 0 to 3, as said below
Outputs:
- best_score: float32 [2048, 512], P(('tile', 'orient'))
- second_score: float32 [2048, 512], P(('tile', 'orient'))
- mean_score: float32 [2048, 512], P(('tile', 'orient'))
- score_variance: float32 [2048, 512], P(('tile', 'orient'))
The draws below stay inside these ranges and needn't reach their ends.
Inputs may be any that keep to these rules, and one draw needn't show every extreme that they name: `defocus_group`: every group is used by some tile.
All inputs are finite; a program needn't handle non-finite values.
Results may differ from the reference program's by a relative error of at most 0.0003.
Values sent between devices are 32-bit elements; how exact they have to be, the bound alone decides.
A program may use at most 128 MiB of HBM per device.

```python
import math
import jax
import jax.numpy as jnp
from jax import lax

TS = 512
TPL = 256
GROUPS = 4
TILES = 4
ORIENTS = 8
ROWS = 2048


def draw_micrograph(key, part):
    key_noise = jax.random.fold_in(key, 0)
    last_tile = max(ROWS // TS - 1, 1)
    fraction = (jnp.arange(ROWS) // TS).astype(jnp.float32) / last_tile
    factor = jnp.exp(math.log(3.0) * fraction)[:, None]
    offset = (0.2 + 0.6 * fraction)[:, None]
    noise_map = jax.random.truncated_normal(key_noise, -4.0, 4.0, (ROWS, TS), jnp.float32)
    return (noise_map * factor + offset).astype(jnp.float32)


def draw_defocus_group(key, part):
    order = jax.random.permutation(jax.random.fold_in(key, 7), TILES)
    return (order % GROUPS).astype(jnp.int32)


def block_levels(own_key, dims, shards, least, largest):
    loudness, own = 1.0, jax.random.fold_in(own_key, 6)
    for dim, blocks in shards:
        draws = jnp.exp(jax.random.uniform(jax.random.fold_in(own, dim), (blocks,), jnp.float32, least / len(shards), largest / len(shards)))
        loudness = loudness * jnp.repeat(draws, dims[dim] // blocks).reshape([-1 if axis == dim else 1 for axis in range(len(dims))])
    return loudness


def gaussian(key, extent, scale, limit, cuts=(), kind=jnp.bfloat16):
    result = scale * jax.random.normal(key, extent, jnp.float32)
    if cuts:
        result = result * block_levels(key, extent, cuts, -0.22, 0.18)
    return jnp.clip(result, -limit, limit).astype(kind)


def setup_inputs(seed: int = 0) -> dict:
    seeds = jax.random.split(jax.random.key(seed), 5)
    return {
        "micrograph": draw_micrograph(jax.random.fold_in(seeds[4], 71), 0),
        "templates": gaussian(seeds[1], (ORIENTS, TPL, TPL), 1.0, 6.0, ((0, 8), (1, 4)), jnp.float32),
        "defocus_values": jnp.clip(jax.random.uniform(seeds[2], (GROUPS,), jnp.float32, 5000.0, 20000.0), 5000.0, 20000.0),
        "defocus_group": draw_defocus_group(jax.random.fold_in(seeds[4], 71), 0),
    }


WAVELENGTH = 0.0197
AMPLITUDE = 0.07

def reference(micrograph, templates, defocus_values, defocus_group):
    margin = TPL // 2
    ext_size = TS + TPL
    pixel_count = ROWS * TS
    centre = jnp.sum(micrograph) / pixel_count
    mean_square = jnp.sum(micrograph * micrograph) / pixel_count
    spread = jnp.sqrt(mean_square - centre * centre + 1e-05)
    normal_image = (micrograph - centre) / spread
    padded = jnp.pad(normal_image, margin)
    centred = templates - lax.optimization_barrier(jnp.mean(templates, axis=(1, 2), keepdims=True))
    root_mean = jnp.sqrt(lax.optimization_barrier(jnp.mean(centred * centred, axis=(1, 2), keepdims=True)) + 1e-06)
    normed = centred / (root_mean * TPL)
    tmpl_spec = jnp.conj(jnp.fft.fft2(jnp.pad(normed, ((0, 0), (0, ext_size - TPL), (0, ext_size - TPL)))))
    positions = jnp.arange(ext_size, dtype=jnp.int32)
    frequency = jnp.where(positions < ext_size // 2, positions, positions - ext_size).astype(jnp.float32) / ext_size
    freq_square = frequency[:, None] ** 2 + frequency[None, :] ** 2

    def one_tile(tile_index):
        window = lax.dynamic_slice(padded, (tile_index * TS, jnp.zeros((), jnp.int32)), (ext_size, ext_size))
        defocus = defocus_values[defocus_group[tile_index]]
        phase_shift = math.pi * WAVELENGTH * defocus * freq_square
        contrast = -(math.sqrt(1.0 - AMPLITUDE * AMPLITUDE) * jnp.sin(phase_shift) + AMPLITUDE * jnp.cos(phase_shift))
        product_spec = jnp.fft.fft2(window)[None] * tmpl_spec * contrast[None]
        scores = jnp.real(jnp.fft.ifft2(product_spec))[:, :TS, :TS]
        ranked = lax.top_k(jnp.moveaxis(scores, 0, -1), 2)[0]
        sum_scores = lax.optimization_barrier(jnp.sum(scores, axis=0))
        squares = lax.optimization_barrier(jnp.sum(scores * scores, axis=0))
        mean_map = sum_scores / ORIENTS
        variance = squares / ORIENTS - mean_map * mean_map
        return (ranked[..., 0], ranked[..., 1], mean_map, variance)
    results = lax.map(one_tile, jnp.arange(TILES, dtype=jnp.int32))
    return (results[0].reshape(ROWS, TS), results[1].reshape(ROWS, TS), results[2].reshape(ROWS, TS), results[3].reshape(ROWS, TS))
```

```python
import functools
import math

import jax
import jax.numpy as jnp
import ml_dtypes
import numpy as np
from jax import lax
from jax.experimental import pallas as pl
from jax.experimental.pallas import tpu as pltpu
from jax.sharding import PartitionSpec as P

TS = 512
TPL = 256
MARGIN = TPL // 2
EXT = TS + TPL
HALF = EXT // 2
FREQS = 400
GROUPS = 2
WAVELENGTH = 0.0197
AMPLITUDE = 0.07
ROOT = math.sqrt(3.0) / 2.0
MESH = pl.DeviceIdType.MESH
VMEM = pl.BlockSpec(memory_space=pltpu.VMEM)


def split_table(table):
    high = table.astype(ml_dtypes.bfloat16)
    low = (table - high.astype(np.float64)).astype(ml_dtypes.bfloat16)
    return high, low


@functools.lru_cache(None)
def tables():
    j, n = np.arange(HALF + 1)[:, None], np.arange(EXT)[None, :]
    angle = 2.0 * np.pi * (j * n % EXT) / EXT
    rows = np.zeros((2 * FREQS, EXT))
    rows[: HALF + 1], rows[FREQS : FREQS + HALF + 1] = np.cos(angle), -np.sin(angle)
    sample, a = np.arange(TPL)[:, None], np.arange(TPL)[None, :]
    cols = []
    for b in range(3):
        angle = 2.0 * np.pi * (sample * (3 * a + b) % EXT) / EXT
        re, im = np.cos(angle), -np.sin(angle)
        cols.append(np.block([[re, im], [-im, re]]))
    p, j = np.arange(TS)[:, None], np.arange(HALF)[None, :]
    angle = 2.0 * np.pi * (p * j % EXT) / EXT
    back_re, back_im = 2.0 * np.cos(angle), -2.0 * np.sin(angle)
    back_re[:, 0] = 1.0
    back_im[:, 0] = (-1.0) ** np.arange(TS)
    back = np.concatenate([back_re, back_im], axis=1)
    return split_table(rows) + split_table(np.stack(cols)) + split_table(back)


def split(value):
    high = value.astype(jnp.bfloat16)
    return high, (value - high.astype(jnp.float32)).astype(jnp.bfloat16)


def dot(a, b, contract=0):
    return lax.dot_general(
        a, b, (((1,), (contract,)), ((), ())), preferred_element_type=jnp.float32
    )


def dot3(a, b, contract=0):
    return dot(a[0], b[0], contract) + (dot(a[0], b[1], contract) + dot(a[1], b[0], contract))


def contrast_vectors(defocus):
    def chi(ids):
        signed = np.where(ids < HALF, ids, ids - EXT) / EXT
        return (math.pi * WAVELENGTH) * defocus * jnp.asarray(signed * signed, jnp.float32)

    k = 3 * np.arange(TPL)[None, :] + np.arange(3)[:, None]
    sign = jnp.asarray((-1.0) ** np.arange(TPL), jnp.float32)[None, :]
    chi_k = chi(k)
    along = jnp.stack([jnp.sin(chi_k) * sign, jnp.cos(chi_k) * sign], axis=1)
    j = np.minimum(np.arange(FREQS), HALF)
    chi_j = chi(j)
    wave = math.sqrt(1.0 - AMPLITUDE * AMPLITUDE)
    factor = -1.0 / (EXT * EXT)
    sin_j, cos_j = jnp.sin(chi_j), jnp.cos(chi_j)
    down = jnp.stack(
        [factor * (wave * cos_j - AMPLITUDE * sin_j), factor * (wave * sin_j + AMPLITUDE * cos_j)]
    )
    return along, down[:, :, None]


def gather_body(n, orients, image_ref, tmpl_ref, win_ref, normed_ref, stats, landed, gath,
                send_sem, recv_sem, tsend_sem, trecv_sem, hsend_sem, hrecv_sem):
    me = lax.axis_index("tile")
    orient = lax.axis_index("orient")
    lanes = orients // GROUPS
    share = TPL // n
    mine = lax.div(orient, lanes)
    partner = lax.rem(orient + lanes, orients)

    barrier = pltpu.get_barrier_semaphore()
    for step in range(n):
        other = lax.rem(me + step, n)
        if step:
            pl.semaphore_signal(barrier, inc=1, device_id={"tile": other, "orient": orient}, device_id_type=MESH)
        pl.semaphore_signal(barrier, inc=1, device_id={"tile": other, "orient": partner}, device_id_type=MESH)
    pl.semaphore_wait(barrier, 2 * n - 1)

    def tmpl_copy(step, away):
        other = lax.rem(me + step, n)
        where = partner if away else orient
        start = pl.multiple_of(me * share, share)
        return pltpu.make_async_remote_copy(
            src_ref=tmpl_ref.at[0],
            dst_ref=gath.at[mine, pl.ds(start, share)],
            send_sem=tsend_sem.at[away, step],
            recv_sem=trecv_sem.at[away, step],
            device_id={"tile": other, "orient": where},
            device_id_type=MESH,
        )

    def halo_copy(up):
        return pltpu.make_async_remote_copy(
            src_ref=image_ref.at[pl.ds(TS - MARGIN if up else 0, MARGIN)],
            dst_ref=landed.at[0 if up else 1],
            send_sem=hsend_sem.at[0 if up else 1],
            recv_sem=hrecv_sem.at[0 if up else 1],
            device_id={"tile": lax.rem(me + (1 if up else n - 1), n), "orient": orient},
            device_id_type=MESH,
        )

    tcopies = [tmpl_copy(s, a) for a in (1, 0) for s in range(n) if s or a]
    for copy in tcopies:
        copy.start()
    halos = [halo_copy(True), halo_copy(False)]
    for copy in halos:
        copy.start()

    image = image_ref[...]
    total = jnp.sum(image)
    squares = jnp.sum(image * image)
    lane = lax.broadcasted_iota(jnp.int32, (8, 128), 1)
    stats[me] = jnp.where(lane == 0, total, jnp.where(lane == 1, squares, 0.0))
    scopies = []
    for step in range(1, n):
        copy = pltpu.make_async_remote_copy(
            src_ref=stats.at[me],
            dst_ref=stats.at[me],
            send_sem=send_sem.at[step],
            recv_sem=recv_sem.at[step],
            device_id={"tile": lax.rem(me + step, n), "orient": orient},
            device_id_type=MESH,
        )
        copy.start()
        scopies.append(copy)
    gath[mine, pl.ds(pl.multiple_of(me * share, share), share)] = tmpl_ref[0]
    for copy in scopies:
        copy.wait()
    sums = stats[0]
    for step in range(1, n):
        sums = sums + stats[step]
    pixels = float(TS * TS * n)
    centre = jnp.sum(jnp.where(lane == 0, sums, 0.0)) / (8.0 * pixels)
    square = jnp.sum(jnp.where(lane == 1, sums, 0.0)) / (8.0 * pixels)
    centre = jnp.full((1, TS), centre, jnp.float32)
    inverse = lax.rsqrt(square - centre * centre + 1e-05)
    win_ref[MARGIN : MARGIN + TS] = (image - centre) * inverse
    for copy in halos:
        copy.wait()
    win_ref[:MARGIN] = jnp.where(me > 0, (landed[0] - centre) * inverse, 0.0)
    win_ref[MARGIN + TS :] = jnp.where(me < n - 1, (landed[1] - centre) * inverse, 0.0)
    for copy in tcopies:
        copy.wait()
    for g in range(GROUPS):
        tmpl = gath[g]
        centred = tmpl - jnp.sum(tmpl) / (TPL * TPL)
        mean_square = jnp.full((1, TPL), jnp.sum(centred * centred) / (TPL * TPL), jnp.float32)
        normed_ref[g] = centred * (lax.rsqrt(mean_square + 1e-06) * (1.0 / TPL))


def score_body(orients, win_ref, normed_ref, along_ref, down_ref, rows_h, rows_l, cols_h, cols_l,
               back_h, back_l, out_ref, half_spec, u_h, u_l, wide, v_h, v_l, backs):
    lanes = orients // GROUPS
    mine = lax.div(lax.axis_index("orient"), lanes)
    part = TS // GROUPS

    half_spec[...] = dot3((rows_h[...], rows_l[...]), split(win_ref[...]))
    re0, re1 = half_spec[:FREQS, :TPL], half_spec[:FREQS, TPL:]
    im0, im1 = half_spec[FREQS:, :TPL], half_spec[FREQS:, TPL:]
    joined = (
        (re0 + re1, im0 + im1),
        (0.5 * re0 + ROOT * im0 - re1, 0.5 * im0 - ROOT * re0 - im1),
        (re1 - 0.5 * re0 + ROOT * im0, im1 - 0.5 * im0 - ROOT * re0),
    )
    for b, (re, im) in enumerate(joined):
        u_h[b, :, :TPL], u_l[b, :, :TPL] = split(re)
        u_h[b, :, TPL:], u_l[b, :, TPL:] = split(im)

    def forward(b, carry):
        spec = dot3((u_h[b], u_l[b]), (cols_h[b], cols_l[b]))
        contrast = along_ref[b, 0:1] * down_ref[0] + along_ref[b, 1:2] * down_ref[1]
        wide[b, :, :TPL] = spec[:, :TPL] * contrast
        wide[b, :, TPL:] = spec[:, TPL:] * contrast
        return carry

    lax.fori_loop(0, 3, forward, 0)

    def one(g, carry):
        first = dot3((rows_h[:, :TPL], rows_l[:, :TPL]), split(normed_ref[g]))
        v_h[:, :TPL], v_l[:, :TPL] = split(first[:FREQS])
        v_h[:, TPL:], v_l[:, TPL:] = split(first[FREQS:])

        def branch(b, carry):
            spec = dot3((v_h[...], v_l[...]), (cols_h[b], cols_l[b]))
            w_re, w_im = wide[b, :, :TPL], wide[b, :, TPL:]
            t_re, t_im = spec[:, :TPL], spec[:, TPL:]
            prod = jnp.concatenate([w_re * t_re + w_im * t_im, w_im * t_re - w_re * t_im], axis=1)
            backs[b] = dot3(split(prod), (cols_h[b], cols_l[b]), 1)
            return carry

        lax.fori_loop(0, 3, branch, 0)
        e_re, e_im = [backs[b, :, :TPL] for b in range(3)], [backs[b, :, TPL:] for b in range(3)]
        sum_re, sum_im = e_re[1] + e_re[2], e_im[1] + e_im[2]
        out_re = jnp.concatenate(
            [e_re[0] + sum_re, e_re[0] - 0.5 * sum_re - ROOT * (e_im[1] - e_im[2])], axis=1
        )
        out_im = jnp.concatenate(
            [e_im[0] + sum_im, e_im[0] - 0.5 * sum_im + ROOT * (e_re[1] - e_re[2])], axis=1
        )
        top = lax.broadcasted_iota(jnp.int32, (HALF, 1), 0) == 0
        out_im = jnp.where(top, out_re[HALF : HALF + 1], out_im[:HALF])
        packed = split(jnp.concatenate([out_re[:HALF], out_im], axis=0))
        own = pl.ds(pl.multiple_of(mine * part, part), part)
        out_ref[g] = dot3((back_h[own], back_l[own]), packed)
        return carry

    lax.fori_loop(0, GROUPS, one, 0)


def merge_body(orients, scores_ref, best_ref, second_ref, mean_ref, var_ref, landed, send_sem, recv_sem):
    lanes = orients // GROUPS
    share = TS // orients
    orient = lax.axis_index("orient")
    group = lax.div(orient, lanes)
    lo = lax.rem(orient, lanes)

    def place(step):
        return group * lanes + lax.rem(lo + step, lanes)

    barrier = pltpu.get_barrier_semaphore()
    for step in range(1, lanes):
        pl.semaphore_signal(barrier, inc=1, device_id={"orient": place(step)}, device_id_type=MESH)
    pl.semaphore_wait(barrier, lanes - 1)
    copies = []
    for g in range(GROUPS):
        for step in range(1, lanes):
            start = pl.multiple_of(lax.rem(lo + step, lanes) * share, share)
            copy = pltpu.make_async_remote_copy(
                src_ref=scores_ref.at[g, pl.ds(start, share)],
                dst_ref=landed.at[g, step],
                send_sem=send_sem.at[g, step],
                recv_sem=recv_sem.at[g, step],
                device_id={"orient": place(step)},
                device_id_type=MESH,
            )
            copy.start()
            copies.append(copy)
    own = pl.ds(pl.multiple_of(lo * share, share), share)
    first, other = scores_ref[0, own], scores_ref[1, own]
    best, second = jnp.maximum(first, other), jnp.minimum(first, other)
    total, squares = first + other, first * first + other * other
    for copy in copies:
        copy.wait()
    for step in range(1, lanes):
        for g in range(GROUPS):
            score = landed[g, step]
            second = jnp.maximum(second, jnp.minimum(best, score))
            best = jnp.maximum(best, score)
            total = total + score
            squares = squares + score * score
    mean = total / orients
    best_ref[...] = best
    second_ref[...] = second
    mean_ref[...] = mean
    var_ref[...] = squares / orients - mean * mean


def per_device(n, orients, micrograph, templates, defocus_values, defocus_group):
    f32, b16 = jnp.float32, jnp.bfloat16
    lanes, share = orients // GROUPS, TS // orients
    group_ids = lax.iota(jnp.int32, defocus_values.shape[0])
    defocus = jnp.sum(jnp.where(group_ids == defocus_group[0], defocus_values, 0.0))
    along, down = contrast_vectors(defocus)
    dma = pltpu.SemaphoreType.DMA
    window, normed = pl.pallas_call(
        functools.partial(gather_body, n, orients),
        out_shape=(
            jax.ShapeDtypeStruct((EXT, TS), f32),
            jax.ShapeDtypeStruct((GROUPS, TPL, TPL), f32),
        ),
        in_specs=[VMEM] * 2,
        out_specs=(VMEM, VMEM),
        scratch_shapes=[
            pltpu.VMEM((n, 8, 128), f32),
            pltpu.VMEM((2, MARGIN, TS), f32),
            pltpu.VMEM((GROUPS, TPL, TPL), f32),
            dma((n,)), dma((n,)), dma((2, n)), dma((2, n)), dma((2,)), dma((2,)),
        ],
        compiler_params=pltpu.CompilerParams(
            collective_id=0, has_side_effects=True, vmem_limit_bytes=16 * 2**20
        ),
        name="gather_normalise",
    )(micrograph, templates)
    scores = pl.pallas_call(
        functools.partial(score_body, orients),
        out_shape=jax.ShapeDtypeStruct((GROUPS, TS // GROUPS, TS), f32),
        in_specs=[VMEM] * 10,
        out_specs=VMEM,
        scratch_shapes=[
            pltpu.VMEM((2 * FREQS, TS), f32),
            pltpu.VMEM((3, FREQS, TS), b16),
            pltpu.VMEM((3, FREQS, TS), b16),
            pltpu.VMEM((3, FREQS, TS), f32),
            pltpu.VMEM((FREQS, TS), b16),
            pltpu.VMEM((FREQS, TS), b16),
            pltpu.VMEM((3, FREQS, TS), f32),
        ],
        compiler_params=pltpu.CompilerParams(vmem_limit_bytes=56 * 2**20),
        name="score",
    )(window, normed, along, down, *(jnp.asarray(t) for t in tables()))
    out = jax.ShapeDtypeStruct((share, TS), f32)
    return pl.pallas_call(
        functools.partial(merge_body, orients),
        out_shape=(out,) * 4,
        in_specs=[VMEM],
        out_specs=(VMEM,) * 4,
        scratch_shapes=[
            pltpu.VMEM((GROUPS, lanes, share, TS), f32),
            dma((GROUPS, lanes)),
            dma((GROUPS, lanes)),
        ],
        compiler_params=pltpu.CompilerParams(
            collective_id=1, has_side_effects=True, vmem_limit_bytes=16 * 2**20
        ),
        name="exchange_merge",
    )(scores)


def solution(mesh):
    placed = (P("tile", None), P("orient", "tile", None), P(), P("tile"))
    return jax.shard_map(
        functools.partial(per_device, mesh.shape["tile"], mesh.shape["orient"]),
        mesh=mesh,
        in_specs=placed,
        out_specs=(P(("tile", "orient"), None),) * 4,
        check_vma=False,
    )
```

```python
import functools
import math

import jax
import jax.numpy as jnp
import ml_dtypes
import numpy as np
from jax import lax
from jax.experimental import pallas as pl
from jax.experimental.pallas import tpu as pltpu
from jax.sharding import PartitionSpec as P

TS = 512
TPL = 256
MARGIN = TPL // 2
EXT = TS + TPL
HALF = EXT // 2
FREQS = 400
GROUPS = 2
WAVELENGTH = 0.0197
AMPLITUDE = 0.07
ROOT = math.sqrt(3.0) / 2.0
MESH = pl.DeviceIdType.MESH
VMEM = pl.BlockSpec(memory_space=pltpu.VMEM)


def split_table(table):
    high = table.astype(ml_dtypes.bfloat16)
    low = (table - high.astype(np.float64)).astype(ml_dtypes.bfloat16)
    return high, low


@functools.lru_cache(None)
def tables():
    j, n = np.arange(HALF + 1)[:, None], np.arange(EXT)[None, :]
    angle = 2.0 * np.pi * (j * n % EXT) / EXT
    rows = np.zeros((2 * FREQS, EXT))
    rows[: HALF + 1], rows[FREQS : FREQS + HALF + 1] = np.cos(angle), -np.sin(angle)
    sample, a = np.arange(TPL)[:, None], np.arange(TPL)[None, :]
    cols = []
    for b in range(3):
        angle = 2.0 * np.pi * (sample * (3 * a + b) % EXT) / EXT
        re, im = np.cos(angle), -np.sin(angle)
        cols.append(np.block([[re, im], [-im, re]]))
    p, j = np.arange(TS)[:, None], np.arange(HALF)[None, :]
    angle = 2.0 * np.pi * (p * j % EXT) / EXT
    back_re, back_im = 2.0 * np.cos(angle), -2.0 * np.sin(angle)
    back_re[:, 0] = 1.0
    back_im[:, 0] = (-1.0) ** np.arange(TS)
    back = np.concatenate([back_re, back_im], axis=1)
    return split_table(rows) + split_table(np.stack(cols)) + split_table(back)


def split(value):
    high = value.astype(jnp.bfloat16)
    return high, (value - high.astype(jnp.float32)).astype(jnp.bfloat16)


def dot(a, b, contract=0):
    return lax.dot_general(
        a, b, (((1,), (contract,)), ((), ())), preferred_element_type=jnp.float32
    )


def dot3(a, b, contract=0):
    return dot(a[0], b[0], contract) + (dot(a[0], b[1], contract) + dot(a[1], b[0], contract))


def circular(turns):
    half = (turns - jnp.round(turns)) * math.pi
    square = half * half
    sine = jnp.full_like(half, 1.0 / math.factorial(13))
    cosine = jnp.full_like(half, -1.0 / math.factorial(14))
    for k in range(5, -1, -1):
        sine = sine * square + (-1.0) ** k / math.factorial(2 * k + 1)
    for k in range(6, -1, -1):
        cosine = cosine * square + (-1.0) ** k / math.factorial(2 * k)
    sine = sine * half
    return 2.0 * sine * cosine, 1.0 - 2.0 * sine * sine


def contrast_vectors(defocus):
    a = lax.broadcasted_iota(jnp.int32, (8, TPL), 1)
    b = lax.broadcasted_iota(jnp.int32, (8, TPL), 0)
    k = 3 * a + b
    k = jnp.where(k < HALF, k, k - EXT).astype(jnp.float32) * (1.0 / EXT)
    j = jnp.minimum(lax.broadcasted_iota(jnp.int32, (FREQS, 128), 0), HALF)
    j = j.astype(jnp.float32) * (1.0 / EXT)
    sign = (1 - 2 * (a & 1)).astype(jnp.float32)
    rate = (WAVELENGTH / 2.0) * defocus
    sin_k, cos_k = circular(rate * (k * k))
    sin_j, cos_j = circular(rate * (j * j))
    wave = math.sqrt(1.0 - AMPLITUDE * AMPLITUDE)
    factor = -1.0 / (EXT * EXT)
    return (
        (sin_k * sign, cos_k * sign),
        (factor * (wave * cos_j - AMPLITUDE * sin_j), factor * (wave * sin_j + AMPLITUDE * cos_j)),
    )


def body(n, orients, values_ref, group_ref, image_ref, tmpl_ref, *rest):
    hbm_tables, rest = rest[:6], rest[6:]
    (out_ref, rows_h, rows_l, cols_h, cols_l, back_h, back_l, stats, halo, gath, win_h, win_l,
     along, down, half_spec, u_h, u_l, wide, v_h, v_l, backs, scores, landed,
     table_sem, stat_send, stat_recv, halo_send, halo_recv, far_send, far_recv,
     near_send, near_recv, pass_send, pass_recv, score_send, score_recv) = rest
    me, orient = lax.axis_index("tile"), lax.axis_index("orient")
    lanes, share, shard = orients // GROUPS, TS // orients, TPL // n
    mine, lo = lax.div(orient, lanes), lax.rem(orient, lanes)
    partner = lax.rem(orient + lanes, orients)
    own_shard = pl.ds(pl.multiple_of(me * shard, shard), shard)

    def tile(step):
        return {"tile": lax.rem(me + step, n), "orient": orient}

    def lane(step):
        return {"tile": me, "orient": mine * lanes + lax.rem(lo + step, lanes)}

    across = {"tile": me, "orient": partner}

    def send(src, dst, send_sem, recv_sem, where):
        copy = pltpu.make_async_remote_copy(
            src_ref=src, dst_ref=dst, send_sem=send_sem, recv_sem=recv_sem,
            device_id=where, device_id_type=MESH,
        )
        copy.start()
        return copy

    barrier = pltpu.get_barrier_semaphore()
    for step in range(1, n):
        pl.semaphore_signal(barrier, inc=1, device_id=tile(step), device_id_type=MESH)
    pl.semaphore_signal(barrier, inc=1, device_id=across, device_id_type=MESH)
    for step in range(1, lanes):
        pl.semaphore_signal(barrier, inc=1, device_id=lane(step), device_id_type=MESH)

    held = (rows_h, rows_l, cols_h, cols_l, back_h, back_l)
    loads = [pltpu.make_async_copy(src, dst, table_sem.at[i])
             for i, (src, dst) in enumerate(zip(hbm_tables, held))]
    for load in loads:
        load.start()

    image = image_ref[...]
    total = jnp.sum(image)
    squares = jnp.sum(image * image)
    spot = lax.broadcasted_iota(jnp.int32, (8, 128), 1)
    stats[me] = jnp.where(spot == 0, total, jnp.where(spot == 1, squares, 0.0))
    gath[mine, own_shard] = tmpl_ref[0]

    pl.semaphore_wait(barrier, (n - 1) + 1 + (lanes - 1))
    stat_copies = [
        send(stats.at[me], stats.at[me], stat_send.at[s], stat_recv.at[s], tile(s))
        for s in range(1, n)
    ]
    halo_copies = [
        send(image_ref.at[pl.ds(TS - MARGIN, MARGIN)], halo.at[0], halo_send.at[0], halo_recv.at[0], tile(1)),
        send(image_ref.at[pl.ds(0, MARGIN)], halo.at[1], halo_send.at[1], halo_recv.at[1], tile(n - 1)),
    ]
    far_copy = send(tmpl_ref.at[0], gath.at[mine, own_shard], far_send, far_recv, across)
    near_copies = [
        send(tmpl_ref.at[0], gath.at[mine, own_shard], near_send.at[s], near_recv.at[s], tile(s))
        for s in range(1, n)
    ]

    wave_along, wave_down = contrast_vectors(values_ref[group_ref[0]])
    for i in range(2):
        along[i] = wave_along[i]
        down[i] = wave_down[i]

    for copy in stat_copies:
        copy.wait()
    sums = stats[0]
    for step in range(1, n):
        sums = sums + stats[step]
    pixels = float(TS * TS * n)
    centre = jnp.sum(jnp.where(spot == 0, sums, 0.0)) / (8.0 * pixels)
    square = jnp.sum(jnp.where(spot == 1, sums, 0.0)) / (8.0 * pixels)
    centre = jnp.full((1, TS), centre, jnp.float32)
    inverse = lax.rsqrt(square - centre * centre + 1e-05)
    inner = pl.ds(MARGIN, TS)
    win_h[inner], win_l[inner] = split((image_ref[...] - centre) * inverse)
    for copy in halo_copies:
        copy.wait()
    for i, (there, where) in enumerate(((me > 0, 0), (me < n - 1, MARGIN + TS))):
        edge = jnp.where(there, (halo[i] - centre) * inverse, 0.0)
        win_h[pl.ds(where, MARGIN)], win_l[pl.ds(where, MARGIN)] = split(edge)

    far_copy.wait()
    far_shard = gath.at[1 - mine, own_shard]
    pass_copies = [
        send(far_shard, far_shard, pass_send.at[s], pass_recv.at[s], tile(s)) for s in range(1, n)
    ]

    for load in loads:
        load.wait()
    half_spec[...] = dot3((rows_h[...], rows_l[...]), (win_h[...], win_l[...]))
    re0, re1 = half_spec[:FREQS, :TPL], half_spec[:FREQS, TPL:]
    im0, im1 = half_spec[FREQS:, :TPL], half_spec[FREQS:, TPL:]
    joined = (
        (re0 + re1, im0 + im1),
        (0.5 * re0 + ROOT * im0 - re1, 0.5 * im0 - ROOT * re0 - im1),
        (re1 - 0.5 * re0 + ROOT * im0, im1 - 0.5 * im0 - ROOT * re0),
    )
    for b, (re, im) in enumerate(joined):
        u_h[b, :, :TPL], u_l[b, :, :TPL] = split(re)
        u_h[b, :, TPL:], u_l[b, :, TPL:] = split(im)

    for b in range(3):
        spec = dot3((u_h[b], u_l[b]), (cols_h[b], cols_l[b]))
        for at in range(0, TPL, 128):
            here = slice(at, at + 128)
            contrast = along[0, b : b + 1, here] * down[0] + along[1, b : b + 1, here] * down[1]
            wide[b, :, at : at + 128] = spec[:, at : at + 128] * contrast
            wide[b, :, TPL + at : TPL + at + 128] = spec[:, TPL + at : TPL + at + 128] * contrast

    score_copies = []
    for turn in range(GROUPS):
        for copy in near_copies if turn == 0 else pass_copies:
            copy.wait()
        tmpl = gath[mine if turn == 0 else 1 - mine]
        centred = tmpl - jnp.sum(tmpl) / (TPL * TPL)
        mean_square = jnp.full((1, TPL), jnp.sum(centred * centred) / (TPL * TPL), jnp.float32)
        normed = centred * (lax.rsqrt(mean_square + 1e-06) * (1.0 / TPL))
        first = dot3((rows_h[:, :TPL], rows_l[:, :TPL]), split(normed))
        v_h[:, :TPL], v_l[:, :TPL] = split(first[:FREQS])
        v_h[:, TPL:], v_l[:, TPL:] = split(first[FREQS:])

        def branch(b, carry):
            spec = dot3((v_h[...], v_l[...]), (cols_h[b], cols_l[b]))
            w_re, w_im = wide[b, :, :TPL], wide[b, :, TPL:]
            t_re, t_im = spec[:, :TPL], spec[:, TPL:]
            prod = jnp.concatenate([w_re * t_re + w_im * t_im, w_im * t_re - w_re * t_im], axis=1)
            backs[b] = dot3(split(prod), (cols_h[b], cols_l[b]), 1)
            return carry

        lax.fori_loop(0, 3, branch, 0)
        e_re, e_im = [backs[b, :, :TPL] for b in range(3)], [backs[b, :, TPL:] for b in range(3)]
        sum_re, sum_im = e_re[1] + e_re[2], e_im[1] + e_im[2]
        out_re = jnp.concatenate(
            [e_re[0] + sum_re, e_re[0] - 0.5 * sum_re - ROOT * (e_im[1] - e_im[2])], axis=1
        )
        out_im = jnp.concatenate(
            [e_im[0] + sum_im, e_im[0] - 0.5 * sum_im + ROOT * (e_re[1] - e_re[2])], axis=1
        )
        top = lax.broadcasted_iota(jnp.int32, (HALF, 1), 0) == 0
        out_im = jnp.where(top, out_re[HALF : HALF + 1], out_im[:HALF])
        packed = split(jnp.concatenate([out_re[:HALF], out_im], axis=0))
        part = TS // GROUPS
        own = pl.ds(pl.multiple_of(mine * part, part), part)
        scores[turn] = dot3((back_h[own], back_l[own]), packed)
        for step in range(1, lanes):
            start = pl.multiple_of(lax.rem(lo + step, lanes) * share, share)
            score_copies.append(send(
                scores.at[turn, pl.ds(start, share)], landed.at[turn, step],
                score_send.at[turn, step], score_recv.at[turn, step], lane(step),
            ))

    own = pl.ds(pl.multiple_of(lo * share, share), share)
    first, other = scores[0, own], scores[1, own]
    best, second = jnp.maximum(first, other), jnp.minimum(first, other)
    total, squares = first + other, first * first + other * other
    for copy in score_copies:
        copy.wait()
    for g in range(GROUPS):
        for step in range(1, lanes):
            score = landed[g, step]
            second = jnp.maximum(second, jnp.minimum(best, score))
            best = jnp.maximum(best, score)
            total = total + score
            squares = squares + score * score
    out_ref[0] = best
    out_ref[1] = second
    out_ref[2] = total
    out_ref[3] = squares


def finish(orients, merged_ref, best_ref, second_ref, mean_ref, var_ref):
    best_ref[...] = merged_ref[0]
    second_ref[...] = merged_ref[1]
    mean = merged_ref[2] / orients
    mean_ref[...] = mean
    var_ref[...] = merged_ref[3] / orients - mean * mean


def per_device(n, orients, micrograph, templates, defocus_values, defocus_group):
    f32, b16 = jnp.float32, jnp.bfloat16
    lanes, share = orients // GROUPS, TS // orients
    dma, vmem = pltpu.SemaphoreType.DMA, pltpu.VMEM
    held = [jnp.asarray(t) for t in tables()]
    smem = pl.BlockSpec(memory_space=pltpu.SMEM)
    anywhere = pl.BlockSpec(memory_space=pl.ANY)
    merged = pl.pallas_call(
        functools.partial(body, n, orients),
        out_shape=jax.ShapeDtypeStruct((4, share, TS), f32),
        in_specs=[smem, smem, VMEM, VMEM] + [anywhere] * 6,
        out_specs=VMEM,
        scratch_shapes=[vmem(t.shape, b16) for t in held] + [
            vmem((n, 8, 128), f32),
            vmem((2, MARGIN, TS), f32),
            vmem((GROUPS, TPL, TPL), f32),
            vmem((EXT, TS), b16),
            vmem((EXT, TS), b16),
            vmem((2, 8, TPL), f32),
            vmem((2, FREQS, 128), f32),
            vmem((2 * FREQS, TS), f32),
            vmem((3, FREQS, TS), b16),
            vmem((3, FREQS, TS), b16),
            vmem((3, FREQS, TS), f32),
            vmem((FREQS, TS), b16),
            vmem((FREQS, TS), b16),
            vmem((3, FREQS, TS), f32),
            vmem((GROUPS, TS // GROUPS, TS), f32),
            vmem((GROUPS, lanes, share, TS), f32),
            dma((6,)),
            dma((n,)), dma((n,)), dma((2,)), dma((2,)), dma, dma,
            dma((n,)), dma((n,)), dma((n,)), dma((n,)),
            dma((GROUPS, lanes)), dma((GROUPS, lanes)),
        ],
        compiler_params=pltpu.CompilerParams(
            collective_id=0, has_side_effects=True, vmem_limit_bytes=56 * 2**20
        ),
        name="match",
    )(defocus_values, defocus_group, micrograph, templates, *held)
    return pl.pallas_call(
        functools.partial(finish, orients),
        out_shape=(jax.ShapeDtypeStruct((share, TS), f32),) * 4,
        in_specs=[VMEM],
        out_specs=(VMEM,) * 4,
        name="finish",
    )(merged)


def solution(mesh):
    placed = (P("tile", None), P("orient", "tile", None), P(), P("tile"))
    return jax.shard_map(
        functools.partial(per_device, mesh.shape["tile"], mesh.shape["orient"]),
        mesh=mesh,
        in_specs=placed,
        out_specs=(P(("tile", "orient"), None),) * 4,
        check_vma=False,
    )
```

```python
import functools
import math

import jax
import jax.numpy as jnp
import ml_dtypes
import numpy as np
from jax import lax
from jax.experimental import pallas as pl
from jax.experimental.pallas import tpu as pltpu
from jax.sharding import PartitionSpec as P

TS = 512
TPL = 256
MARGIN = TPL // 2
EXT = TS + TPL
HALF = EXT // 2
FREQS = 400
GROUPS = 2
WAVELENGTH = 0.0197
AMPLITUDE = 0.07
ROOT = math.sqrt(3.0) / 2.0
MESH = pl.DeviceIdType.MESH
VMEM = pl.BlockSpec(memory_space=pltpu.VMEM)


def split_table(table):
    high = table.astype(ml_dtypes.bfloat16)
    low = (table - high.astype(np.float64)).astype(ml_dtypes.bfloat16)
    return high, low


@functools.lru_cache(None)
def tables():
    j, n = np.arange(HALF + 1)[:, None], np.arange(EXT)[None, :]
    angle = 2.0 * np.pi * (j * n % EXT) / EXT
    rows = np.zeros((2 * FREQS, EXT))
    rows[: HALF + 1], rows[FREQS : FREQS + HALF + 1] = np.cos(angle), -np.sin(angle)
    sample, a = np.arange(TPL)[:, None], np.arange(TPL)[None, :]
    cols = []
    for b in range(3):
        angle = 2.0 * np.pi * (sample * (3 * a + b) % EXT) / EXT
        re, im = np.cos(angle), -np.sin(angle)
        cols.append(np.block([[re, im], [-im, re]]))
    p, j = np.arange(TS)[:, None], np.arange(HALF)[None, :]
    angle = 2.0 * np.pi * (p * j % EXT) / EXT
    back_re, back_im = 2.0 * np.cos(angle), -2.0 * np.sin(angle)
    back_re[:, 0] = 1.0
    back_im[:, 0] = (-1.0) ** np.arange(TS)
    back = np.concatenate([back_re, back_im], axis=1)
    return split_table(rows) + split_table(np.stack(cols)) + split_table(back)


def split(value):
    high = value.astype(jnp.bfloat16)
    return high, (value - high.astype(jnp.float32)).astype(jnp.bfloat16)


def dot(a, b, contract=0):
    return lax.dot_general(
        a, b, (((1,), (contract,)), ((), ())), preferred_element_type=jnp.float32
    )


def dot3(a, b, contract=0):
    left = jnp.concatenate([a[0], a[1], a[0]], axis=1)
    right = jnp.concatenate([b[0], b[0], b[1]], axis=contract)
    return dot(left, right, contract)


def circular(turns):
    half = (turns - jnp.round(turns)) * math.pi
    square = half * half
    sine = jnp.full_like(half, 1.0 / math.factorial(13))
    cosine = jnp.full_like(half, -1.0 / math.factorial(14))
    for k in range(5, -1, -1):
        sine = sine * square + (-1.0) ** k / math.factorial(2 * k + 1)
    for k in range(6, -1, -1):
        cosine = cosine * square + (-1.0) ** k / math.factorial(2 * k)
    sine = sine * half
    return 2.0 * sine * cosine, 1.0 - 2.0 * sine * sine


def contrast_vectors(defocus):
    a = lax.broadcasted_iota(jnp.int32, (8, TPL), 1)
    b = lax.broadcasted_iota(jnp.int32, (8, TPL), 0)
    k = 3 * a + b
    k = jnp.where(k < HALF, k, k - EXT).astype(jnp.float32) * (1.0 / EXT)
    j = jnp.minimum(lax.broadcasted_iota(jnp.int32, (FREQS, 128), 0), HALF)
    j = j.astype(jnp.float32) * (1.0 / EXT)
    sign = (1 - 2 * (a & 1)).astype(jnp.float32)
    rate = (WAVELENGTH / 2.0) * defocus
    sin_k, cos_k = circular(rate * (k * k))
    sin_j, cos_j = circular(rate * (j * j))
    wave = math.sqrt(1.0 - AMPLITUDE * AMPLITUDE)
    factor = -1.0 / (EXT * EXT)
    return (
        (sin_k * sign, cos_k * sign),
        (factor * (wave * cos_j - AMPLITUDE * sin_j), factor * (wave * sin_j + AMPLITUDE * cos_j)),
    )


def body(n, orients, values_ref, group_ref, image_ref, tmpl_ref, *rest):
    hbm_tables, rest = rest[:6], rest[6:]
    (out_ref, rows_h, rows_l, cols_h, cols_l, back_h, back_l, stats, halo, gath, win_h, win_l,
     along, down, half_spec, u_h, u_l, wide, v_h, v_l, backs, scores, landed,
     table_sem, stat_send, stat_recv, halo_send, halo_recv, far_send, far_recv,
     near_send, near_recv, pass_send, pass_recv, score_send, score_recv) = rest
    me, orient = lax.axis_index("tile"), lax.axis_index("orient")
    lanes, share, shard = orients // GROUPS, TS // orients, TPL // n
    mine, lo = lax.div(orient, lanes), lax.rem(orient, lanes)
    partner = lax.rem(orient + lanes, orients)
    own_shard = pl.ds(pl.multiple_of(me * shard, shard), shard)

    def tile(step):
        return {"tile": lax.rem(me + step, n), "orient": orient}

    def lane(step):
        return {"tile": me, "orient": mine * lanes + lax.rem(lo + step, lanes)}

    across = {"tile": me, "orient": partner}

    def send(src, dst, send_sem, recv_sem, where):
        copy = pltpu.make_async_remote_copy(
            src_ref=src, dst_ref=dst, send_sem=send_sem, recv_sem=recv_sem,
            device_id=where, device_id_type=MESH,
        )
        copy.start()
        return copy

    barrier = pltpu.get_barrier_semaphore()
    for step in range(1, n):
        pl.semaphore_signal(barrier, inc=1, device_id=tile(step), device_id_type=MESH)
    pl.semaphore_signal(barrier, inc=1, device_id=across, device_id_type=MESH)
    for step in range(1, lanes):
        pl.semaphore_signal(barrier, inc=1, device_id=lane(step), device_id_type=MESH)

    held = (rows_h, rows_l, cols_h, cols_l, back_h, back_l)
    loads = [pltpu.make_async_copy(src, dst, table_sem.at[i])
             for i, (src, dst) in enumerate(zip(hbm_tables, held))]
    for load in loads:
        load.start()

    image = image_ref[...]
    total = jnp.sum(image)
    squares = jnp.sum(image * image)
    spot = lax.broadcasted_iota(jnp.int32, (8, 128), 1)
    stats[me] = jnp.where(spot == 0, total, jnp.where(spot == 1, squares, 0.0))
    gath[mine, own_shard] = tmpl_ref[0]

    pl.semaphore_wait(barrier, (n - 1) + 1 + (lanes - 1))
    stat_copies = [
        send(stats.at[me], stats.at[me], stat_send.at[s], stat_recv.at[s], tile(s))
        for s in range(1, n)
    ]
    halo_copies = [
        send(image_ref.at[pl.ds(TS - MARGIN, MARGIN)], halo.at[0], halo_send.at[0], halo_recv.at[0], tile(1)),
        send(image_ref.at[pl.ds(0, MARGIN)], halo.at[1], halo_send.at[1], halo_recv.at[1], tile(n - 1)),
    ]
    far_copy = send(tmpl_ref.at[0], gath.at[mine, own_shard], far_send, far_recv, across)
    near_copies = [
        send(tmpl_ref.at[0], gath.at[mine, own_shard], near_send.at[s], near_recv.at[s], tile(s))
        for s in range(1, n)
    ]

    wave_along, wave_down = contrast_vectors(values_ref[group_ref[0]])
    for i in range(2):
        along[i] = wave_along[i]
        down[i] = wave_down[i]

    for copy in stat_copies:
        copy.wait()
    sums = stats[0]
    for step in range(1, n):
        sums = sums + stats[step]
    pixels = float(TS * TS * n)
    centre = jnp.sum(jnp.where(spot == 0, sums, 0.0)) / (8.0 * pixels)
    square = jnp.sum(jnp.where(spot == 1, sums, 0.0)) / (8.0 * pixels)
    centre = jnp.full((1, TS), centre, jnp.float32)
    inverse = lax.rsqrt(square - centre * centre + 1e-05)
    inner = pl.ds(MARGIN, TS)
    win_h[inner], win_l[inner] = split((image_ref[...] - centre) * inverse)
    for copy in halo_copies:
        copy.wait()
    for i, (there, where) in enumerate(((me > 0, 0), (me < n - 1, MARGIN + TS))):
        edge = jnp.where(there, (halo[i] - centre) * inverse, 0.0)
        win_h[pl.ds(where, MARGIN)], win_l[pl.ds(where, MARGIN)] = split(edge)

    far_copy.wait()
    far_shard = gath.at[1 - mine, own_shard]
    pass_copies = [
        send(far_shard, far_shard, pass_send.at[s], pass_recv.at[s], tile(s)) for s in range(1, n)
    ]

    for load in loads:
        load.wait()
    half_spec[...] = dot3((rows_h[...], rows_l[...]), (win_h[...], win_l[...]))
    re0, re1 = half_spec[:FREQS, :TPL], half_spec[:FREQS, TPL:]
    im0, im1 = half_spec[FREQS:, :TPL], half_spec[FREQS:, TPL:]
    joined = (
        (re0 + re1, im0 + im1),
        (0.5 * re0 + ROOT * im0 - re1, 0.5 * im0 - ROOT * re0 - im1),
        (re1 - 0.5 * re0 + ROOT * im0, im1 - 0.5 * im0 - ROOT * re0),
    )
    for b, (re, im) in enumerate(joined):
        u_h[b, :, :TPL], u_l[b, :, :TPL] = split(re)
        u_h[b, :, TPL:], u_l[b, :, TPL:] = split(im)

    for b in range(3):
        spec = dot3((u_h[b], u_l[b]), (cols_h[b], cols_l[b]))
        for at in range(0, TPL, 128):
            here = slice(at, at + 128)
            contrast = along[0, b : b + 1, here] * down[0] + along[1, b : b + 1, here] * down[1]
            wide[b, :, at : at + 128] = spec[:, at : at + 128] * contrast
            wide[b, :, TPL + at : TPL + at + 128] = spec[:, TPL + at : TPL + at + 128] * contrast

    score_copies = []
    for turn in range(GROUPS):
        for copy in near_copies if turn == 0 else pass_copies:
            copy.wait()
        tmpl = gath[mine if turn == 0 else 1 - mine]
        centred = tmpl - jnp.sum(tmpl) / (TPL * TPL)
        mean_square = jnp.full((1, TPL), jnp.sum(centred * centred) / (TPL * TPL), jnp.float32)
        normed = centred * (lax.rsqrt(mean_square + 1e-06) * (1.0 / TPL))
        first = dot3((rows_h[:, :TPL], rows_l[:, :TPL]), split(normed))
        v_h[:, :TPL], v_l[:, :TPL] = split(first[:FREQS])
        v_h[:, TPL:], v_l[:, TPL:] = split(first[FREQS:])

        def branch(b, carry):
            spec = dot3((v_h[...], v_l[...]), (cols_h[b], cols_l[b]))
            w_re, w_im = wide[b, :, :TPL], wide[b, :, TPL:]
            t_re, t_im = spec[:, :TPL], spec[:, TPL:]
            prod = jnp.concatenate([w_re * t_re + w_im * t_im, w_im * t_re - w_re * t_im], axis=1)
            backs[b] = dot3(split(prod), (cols_h[b], cols_l[b]), 1)
            return carry

        lax.fori_loop(0, 3, branch, 0)
        e_re, e_im = [backs[b, :, :TPL] for b in range(3)], [backs[b, :, TPL:] for b in range(3)]
        sum_re, sum_im = e_re[1] + e_re[2], e_im[1] + e_im[2]
        out_re = jnp.concatenate(
            [e_re[0] + sum_re, e_re[0] - 0.5 * sum_re - ROOT * (e_im[1] - e_im[2])], axis=1
        )
        out_im = jnp.concatenate(
            [e_im[0] + sum_im, e_im[0] - 0.5 * sum_im + ROOT * (e_re[1] - e_re[2])], axis=1
        )
        top = lax.broadcasted_iota(jnp.int32, (HALF, 1), 0) == 0
        out_im = jnp.where(top, out_re[HALF : HALF + 1], out_im[:HALF])
        packed = split(jnp.concatenate([out_re[:HALF], out_im], axis=0))
        part = TS // GROUPS
        own = pl.ds(pl.multiple_of(mine * part, part), part)
        scores[turn] = dot3((back_h[own], back_l[own]), packed)
        for step in range(1, lanes):
            start = pl.multiple_of(lax.rem(lo + step, lanes) * share, share)
            score_copies.append(send(
                scores.at[turn, pl.ds(start, share)], landed.at[turn, step],
                score_send.at[turn, step], score_recv.at[turn, step], lane(step),
            ))

    own = pl.ds(pl.multiple_of(lo * share, share), share)
    first, other = scores[0, own], scores[1, own]
    best, second = jnp.maximum(first, other), jnp.minimum(first, other)
    total, squares = first + other, first * first + other * other
    for copy in score_copies:
        copy.wait()
    for g in range(GROUPS):
        for step in range(1, lanes):
            score = landed[g, step]
            second = jnp.maximum(second, jnp.minimum(best, score))
            best = jnp.maximum(best, score)
            total = total + score
            squares = squares + score * score
    out_ref[0] = best
    out_ref[1] = second
    out_ref[2] = total
    out_ref[3] = squares


def finish(orients, merged_ref, best_ref, second_ref, mean_ref, var_ref):
    best_ref[...] = merged_ref[0]
    second_ref[...] = merged_ref[1]
    mean = merged_ref[2] / orients
    mean_ref[...] = mean
    var_ref[...] = merged_ref[3] / orients - mean * mean


def per_device(n, orients, micrograph, templates, defocus_values, defocus_group):
    f32, b16 = jnp.float32, jnp.bfloat16
    lanes, share = orients // GROUPS, TS // orients
    dma, vmem = pltpu.SemaphoreType.DMA, pltpu.VMEM
    held = [jnp.asarray(t) for t in tables()]
    smem = pl.BlockSpec(memory_space=pltpu.SMEM)
    anywhere = pl.BlockSpec(memory_space=pl.ANY)
    merged = pl.pallas_call(
        functools.partial(body, n, orients),
        out_shape=jax.ShapeDtypeStruct((4, share, TS), f32),
        in_specs=[smem, smem, VMEM, VMEM] + [anywhere] * 6,
        out_specs=VMEM,
        scratch_shapes=[vmem(t.shape, b16) for t in held] + [
            vmem((n, 8, 128), f32),
            vmem((2, MARGIN, TS), f32),
            vmem((GROUPS, TPL, TPL), f32),
            vmem((EXT, TS), b16),
            vmem((EXT, TS), b16),
            vmem((2, 8, TPL), f32),
            vmem((2, FREQS, 128), f32),
            vmem((2 * FREQS, TS), f32),
            vmem((3, FREQS, TS), b16),
            vmem((3, FREQS, TS), b16),
            vmem((3, FREQS, TS), f32),
            vmem((FREQS, TS), b16),
            vmem((FREQS, TS), b16),
            vmem((3, FREQS, TS), f32),
            vmem((GROUPS, TS // GROUPS, TS), f32),
            vmem((GROUPS, lanes, share, TS), f32),
            dma((6,)),
            dma((n,)), dma((n,)), dma((2,)), dma((2,)), dma, dma,
            dma((n,)), dma((n,)), dma((n,)), dma((n,)),
            dma((GROUPS, lanes)), dma((GROUPS, lanes)),
        ],
        compiler_params=pltpu.CompilerParams(
            collective_id=0, has_side_effects=True, vmem_limit_bytes=56 * 2**20
        ),
        name="match",
    )(defocus_values, defocus_group, micrograph, templates, *held)
    return pl.pallas_call(
        functools.partial(finish, orients),
        out_shape=(jax.ShapeDtypeStruct((share, TS), f32),) * 4,
        in_specs=[VMEM],
        out_specs=(VMEM,) * 4,
        name="finish",
    )(merged)


def solution(mesh):
    placed = (P("tile", None), P("orient", "tile", None), P(), P("tile"))
    return jax.shard_map(
        functools.partial(per_device, mesh.shape["tile"], mesh.shape["orient"]),
        mesh=mesh,
        in_specs=placed,
        out_specs=(P(("tile", "orient"), None),) * 4,
        check_vma=False,
    )
```

```python
import functools
import math

import jax
import jax.numpy as jnp
import ml_dtypes
import numpy as np
from jax import lax
from jax.experimental import pallas as pl
from jax.experimental.pallas import tpu as pltpu
from jax.sharding import PartitionSpec as P

TS = 512
TPL = 256
MARGIN = TPL // 2
EXT = TS + TPL
HALF = EXT // 2
FREQS = 400
GROUPS = 2
WAVELENGTH = 0.0197
AMPLITUDE = 0.07
ROOT = math.sqrt(3.0) / 2.0
RADIX = 6
SUB = EXT // RADIX
MESH = pl.DeviceIdType.MESH
VMEM = pl.BlockSpec(memory_space=pltpu.VMEM)


def split_table(table):
    high = table.astype(ml_dtypes.bfloat16)
    low = (table - high.astype(np.float64)).astype(ml_dtypes.bfloat16)
    return high, low


@functools.lru_cache(None)
def tables():
    j, n = np.arange(HALF + 1)[:, None], np.arange(EXT)[None, :]
    angle = 2.0 * np.pi * (j * n % EXT) / EXT
    rows = np.zeros((2 * FREQS, EXT))
    rows[: HALF + 1], rows[FREQS : FREQS + HALF + 1] = np.cos(angle), -np.sin(angle)
    own = np.repeat(rows[:, MARGIN : MARGIN + TS].sum(axis=1, keepdims=True), 128, axis=1)
    sample, a = np.arange(SUB)[:, None], np.arange(SUB)[None, :]
    cols = []
    for b in range(RADIX):
        angle = 2.0 * np.pi * (sample * (RADIX * a + b) % EXT) / EXT
        re, im = np.cos(angle), -np.sin(angle)
        cols.append(np.block([[re, im], [-im, re]]))
    p, j = np.arange(TS)[:, None], np.arange(HALF)[None, :]
    angle = 2.0 * np.pi * (p * j % EXT) / EXT
    back_re, back_im = 2.0 * np.cos(angle), -2.0 * np.sin(angle)
    back_re[:, 0] = 1.0
    back_im[:, 0] = (-1.0) ** np.arange(TS)
    back = np.concatenate([back_re, back_im], axis=1)
    return split_table(rows) + split_table(np.stack(cols)) + split_table(back) + (own.astype(np.float32),)


def split(value):
    high = value.astype(jnp.bfloat16)
    return high, (value - high.astype(jnp.float32)).astype(jnp.bfloat16)


def dot(a, b, contract=0):
    return lax.dot_general(
        a, b, (((1,), (contract,)), ((), ())), preferred_element_type=jnp.float32
    )


def dot3(a, b, contract=0):
    left = jnp.concatenate([a[0], a[1], a[0]], axis=1)
    right = jnp.concatenate([b[0], b[0], b[1]], axis=contract)
    return dot(left, right, contract)


def turned(x, way):
    re, im = x
    return (way * ROOT) * im - 0.5 * re, (-way * ROOT) * re - 0.5 * im


def plus(x, y):
    return x[0] + y[0], x[1] + y[1]


def minus(x, y):
    return x[0] - y[0], x[1] - y[1]


def three(x, y, z):
    total, apart = plus(y, z), minus(y, z)
    middle = x[0] - 0.5 * total[0], x[1] - 0.5 * total[1]
    side = ROOT * apart[1], -ROOT * apart[0]
    return plus(x, total), plus(middle, side), minus(middle, side)


def circular(turns):
    half = (turns - jnp.round(turns)) * math.pi
    square = half * half
    sine = jnp.full_like(half, 1.0 / math.factorial(13))
    cosine = jnp.full_like(half, -1.0 / math.factorial(14))
    for k in range(5, -1, -1):
        sine = sine * square + (-1.0) ** k / math.factorial(2 * k + 1)
    for k in range(6, -1, -1):
        cosine = cosine * square + (-1.0) ** k / math.factorial(2 * k)
    sine = sine * half
    return 2.0 * sine * cosine, 1.0 - 2.0 * sine * sine


def contrast_vectors(defocus):
    a = lax.broadcasted_iota(jnp.int32, (8, SUB), 1)
    b = lax.broadcasted_iota(jnp.int32, (8, SUB), 0)
    k = RADIX * a + b
    k = jnp.where(k < HALF, k, k - EXT).astype(jnp.float32) * (1.0 / EXT)
    j = jnp.minimum(lax.broadcasted_iota(jnp.int32, (FREQS, 128), 0), HALF)
    j = j.astype(jnp.float32) * (1.0 / EXT)
    rate = (WAVELENGTH / 2.0) * defocus
    sin_k, cos_k = circular(rate * (k * k))
    sin_j, cos_j = circular(rate * (j * j))
    wave = math.sqrt(1.0 - AMPLITUDE * AMPLITUDE)
    factor = -1.0 / (EXT * EXT)
    return (
        (sin_k, cos_k),
        (factor * (wave * cos_j - AMPLITUDE * sin_j), factor * (wave * sin_j + AMPLITUDE * cos_j)),
    )


def body(n, orients, values_ref, group_ref, image_ref, tmpl_ref, *rest):
    hbm_tables, rest = rest[:7], rest[7:]
    (out_ref, rows_h, rows_l, cols_h, cols_l, back_h, back_l, own_sum, stats, halo, gath,
     along, down, half_spec, u_h, u_l, wide, v_h, v_l, backs, scores, landed,
     table_sem, stat_send, stat_recv, halo_send, halo_recv, far_send, far_recv,
     near_send, near_recv, pass_send, pass_recv, score_send, score_recv) = rest
    me, orient = lax.axis_index("tile"), lax.axis_index("orient")
    lanes, share, shard = orients // GROUPS, TS // orients, TPL // n
    mine, lo = lax.div(orient, lanes), lax.rem(orient, lanes)
    partner = lax.rem(orient + lanes, orients)
    own_shard = pl.ds(pl.multiple_of(me * shard, shard), shard)

    def tile(step):
        return {"tile": lax.rem(me + step, n), "orient": orient}

    def lane(step):
        return {"tile": me, "orient": mine * lanes + lax.rem(lo + step, lanes)}

    across = {"tile": me, "orient": partner}

    def send(src, dst, send_sem, recv_sem, where):
        copy = pltpu.make_async_remote_copy(
            src_ref=src, dst_ref=dst, send_sem=send_sem, recv_sem=recv_sem,
            device_id=where, device_id_type=MESH,
        )
        copy.start()
        return copy

    barrier = pltpu.get_barrier_semaphore()
    for step in range(1, n):
        pl.semaphore_signal(barrier, inc=1, device_id=tile(step), device_id_type=MESH)
    pl.semaphore_signal(barrier, inc=1, device_id=across, device_id_type=MESH)
    for step in range(1, lanes):
        pl.semaphore_signal(barrier, inc=1, device_id=lane(step), device_id_type=MESH)

    held = (rows_h, rows_l, cols_h, cols_l, back_h, back_l, own_sum)
    loads = [pltpu.make_async_copy(src, dst, table_sem.at[i])
             for i, (src, dst) in enumerate(zip(hbm_tables, held))]
    for load in loads:
        load.start()

    image = image_ref[...]
    total = jnp.sum(image)
    squares = jnp.sum(image * image)
    spot = lax.broadcasted_iota(jnp.int32, (8, 128), 1)
    stats[me] = jnp.where(spot == 0, total, jnp.where(spot == 1, squares, 0.0))
    gath[mine, own_shard] = tmpl_ref[0]

    pl.semaphore_wait(barrier, (n - 1) + 1 + (lanes - 1))
    stat_copies = [
        send(stats.at[me], stats.at[me], stat_send.at[s], stat_recv.at[s], tile(s))
        for s in range(1, n)
    ]
    halo_copies = [
        send(image_ref.at[pl.ds(TS - MARGIN, MARGIN)], halo.at[0], halo_send.at[0], halo_recv.at[0], tile(1)),
        send(image_ref.at[pl.ds(0, MARGIN)], halo.at[1], halo_send.at[1], halo_recv.at[1], tile(n - 1)),
    ]
    far_copy = send(tmpl_ref.at[0], gath.at[mine, own_shard], far_send, far_recv, across)
    near_copies = [
        send(tmpl_ref.at[0], gath.at[mine, own_shard], near_send.at[s], near_recv.at[s], tile(s))
        for s in range(1, n)
    ]

    wave_along, wave_down = contrast_vectors(values_ref[group_ref[0]])
    for i in range(2):
        along[i] = wave_along[i]

    local = jnp.full((1, TS), total, jnp.float32) * (1.0 / (TS * TS))
    loads[0].wait()
    loads[1].wait()
    inner = slice(MARGIN, MARGIN + TS)
    half_spec[...] = dot3((rows_h[:, inner], rows_l[:, inner]), split(image_ref[...] - local))

    for copy in stat_copies:
        copy.wait()
    sums = stats[0]
    for step in range(1, n):
        sums = sums + stats[step]
    pixels = float(TS * TS * n)
    centre = jnp.sum(jnp.where(spot == 0, sums, 0.0)) / (8.0 * pixels)
    square = jnp.sum(jnp.where(spot == 1, sums, 0.0)) / (8.0 * pixels)
    centre = jnp.full((1, TS), centre, jnp.float32)
    inverse = lax.rsqrt(square - centre * centre + 1e-05)
    for i in range(2):
        down[i] = wave_down[i] * inverse[:, :128]
    for copy in halo_copies:
        copy.wait()
    before = jnp.where(me > 0, halo[0] - centre, 0.0)
    after = jnp.where(me < n - 1, halo[1] - centre, 0.0)

    far_copy.wait()
    far_shard = gath.at[1 - mine, own_shard]
    pass_copies = [
        send(far_shard, far_shard, pass_send.at[s], pass_recv.at[s], tile(s)) for s in range(1, n)
    ]

    edges = [jnp.concatenate([t[:, :MARGIN], t[:, MARGIN + TS :]], axis=1) for t in (rows_h, rows_l)]
    edge_spec = dot3(edges, split(jnp.concatenate([before, after], axis=0)))
    for load in loads[2:]:
        load.wait()
    shift = own_sum[...] * (local - centre)[:, :128]
    block = []
    for m in range(TS // SUB):
        here = slice(m * SUB, (m + 1) * SUB)
        full = half_spec[:, here] + edge_spec[:, here] + shift
        block.append((full[:FREQS], full[FREQS:]))
    even = three(block[2], plus(block[0], block[3]), block[1])
    flip = (-block[1][0], -block[1][1])
    odd = three(block[2], minus(block[0], block[3]), flip)
    odd = [(-re, -im) for re, im in odd]
    for b, part in enumerate((even[0], odd[2], even[1], odd[0], even[2], odd[1])):
        u_h[b, :, :SUB], u_l[b, :, :SUB] = split(part[0])
        u_h[b, :, SUB:], u_l[b, :, SUB:] = split(part[1])

    for b in range(RADIX):
        spec = dot3((u_h[b], u_l[b]), (cols_h[b], cols_l[b]))
        contrast = along[0, b : b + 1] * down[0] + along[1, b : b + 1] * down[1]
        wide[b, :, :SUB] = spec[:, :SUB] * contrast
        wide[b, :, SUB:] = spec[:, SUB:] * contrast

    score_copies = []
    for turn in range(GROUPS):
        for copy in near_copies if turn == 0 else pass_copies:
            copy.wait()
        tmpl = gath[mine if turn == 0 else 1 - mine]
        centred = tmpl - jnp.sum(tmpl) / (TPL * TPL)
        mean_square = jnp.full((1, TPL), jnp.sum(centred * centred) / (TPL * TPL), jnp.float32)
        normed = centred * (lax.rsqrt(mean_square + 1e-06) * (1.0 / TPL))
        first = dot3((rows_h[:, :TPL], rows_l[:, :TPL]), split(normed))
        near = first[:FREQS, :SUB], first[FREQS:, :SUB]
        far = first[:FREQS, SUB:], first[FREQS:, SUB:]
        once, twice = turned(far, 1), turned(far, -1)
        parts = (plus(near, far), minus(near, twice), plus(near, once),
                 minus(near, far), plus(near, twice), minus(near, once))
        for b, (re, im) in enumerate(parts):
            v_h[b, :, :SUB], v_l[b, :, :SUB] = split(re)
            v_h[b, :, SUB:], v_l[b, :, SUB:] = split(im)

        for b in range(RADIX):
            spec = dot3((v_h[b], v_l[b]), (cols_h[b], cols_l[b]))
            w_re, w_im = wide[b, :, :SUB], wide[b, :, SUB:]
            t_re, t_im = spec[:, :SUB], spec[:, SUB:]
            prod = jnp.concatenate([w_re * t_re + w_im * t_im, w_im * t_re - w_re * t_im], axis=1)
            backs[b] = dot3(split(prod), (cols_h[b], cols_l[b]), 1)

        e = [(backs[b, :, :SUB], backs[b, :, SUB:]) for b in range(RADIX)]
        even = three(e[0], e[2], e[4])
        odd = three(e[3], e[5], e[1])
        outs = plus(even[0], odd[0]), minus(even[2], odd[2]), plus(even[1], odd[1]), minus(even[0], odd[0])
        out_re = jnp.concatenate([re for re, _ in outs], axis=1)
        out_im = jnp.concatenate([im for _, im in outs], axis=1)
        top = lax.broadcasted_iota(jnp.int32, (HALF, 1), 0) == 0
        out_im = jnp.where(top, out_re[HALF : HALF + 1], out_im[:HALF])
        packed = split(jnp.concatenate([out_re[:HALF], out_im], axis=0))
        part = TS // GROUPS
        own = pl.ds(pl.multiple_of(mine * part, part), part)
        scores[turn] = dot3((back_h[own], back_l[own]), packed)
        for step in range(1, lanes):
            start = pl.multiple_of(lax.rem(lo + step, lanes) * share, share)
            score_copies.append(send(
                scores.at[turn, pl.ds(start, share)], landed.at[turn, step],
                score_send.at[turn, step], score_recv.at[turn, step], lane(step),
            ))

    own = pl.ds(pl.multiple_of(lo * share, share), share)
    first, other = scores[0, own], scores[1, own]
    best, second = jnp.maximum(first, other), jnp.minimum(first, other)
    total, squares = first + other, first * first + other * other
    for copy in score_copies:
        copy.wait()
    for g in range(GROUPS):
        for step in range(1, lanes):
            score = landed[g, step]
            second = jnp.maximum(second, jnp.minimum(best, score))
            best = jnp.maximum(best, score)
            total = total + score
            squares = squares + score * score
    out_ref[0] = best
    out_ref[1] = second
    out_ref[2] = total
    out_ref[3] = squares


def finish(orients, merged_ref, best_ref, second_ref, mean_ref, var_ref):
    best_ref[...] = merged_ref[0]
    second_ref[...] = merged_ref[1]
    mean = merged_ref[2] / orients
    mean_ref[...] = mean
    var_ref[...] = merged_ref[3] / orients - mean * mean


def per_device(n, orients, micrograph, templates, defocus_values, defocus_group):
    f32, b16 = jnp.float32, jnp.bfloat16
    lanes, share = orients // GROUPS, TS // orients
    dma, vmem = pltpu.SemaphoreType.DMA, pltpu.VMEM
    held = [jnp.asarray(t) for t in tables()]
    smem = pl.BlockSpec(memory_space=pltpu.SMEM)
    anywhere = pl.BlockSpec(memory_space=pl.ANY)
    merged = pl.pallas_call(
        functools.partial(body, n, orients),
        out_shape=jax.ShapeDtypeStruct((4, share, TS), f32),
        in_specs=[smem, smem, VMEM, VMEM] + [anywhere] * 7,
        out_specs=VMEM,
        scratch_shapes=[vmem(t.shape, t.dtype) for t in held] + [
            vmem((n, 8, 128), f32),
            vmem((2, MARGIN, TS), f32),
            vmem((GROUPS, TPL, TPL), f32),
            vmem((2, 8, SUB), f32),
            vmem((2, FREQS, 128), f32),
            vmem((2 * FREQS, TS), f32),
            vmem((RADIX, FREQS, 2 * SUB), b16),
            vmem((RADIX, FREQS, 2 * SUB), b16),
            vmem((RADIX, FREQS, 2 * SUB), f32),
            vmem((RADIX, FREQS, 2 * SUB), b16),
            vmem((RADIX, FREQS, 2 * SUB), b16),
            vmem((RADIX, FREQS, 2 * SUB), f32),
            vmem((GROUPS, TS // GROUPS, TS), f32),
            vmem((GROUPS, lanes, share, TS), f32),
            dma((7,)),
            dma((n,)), dma((n,)), dma((2,)), dma((2,)), dma, dma,
            dma((n,)), dma((n,)), dma((n,)), dma((n,)),
            dma((GROUPS, lanes)), dma((GROUPS, lanes)),
        ],
        compiler_params=pltpu.CompilerParams(
            collective_id=0, has_side_effects=True, vmem_limit_bytes=56 * 2**20
        ),
        name="match",
    )(defocus_values, defocus_group, micrograph, templates, *held)
    return pl.pallas_call(
        functools.partial(finish, orients),
        out_shape=(jax.ShapeDtypeStruct((share, TS), f32),) * 4,
        in_specs=[VMEM],
        out_specs=(VMEM,) * 4,
        name="finish",
    )(merged)


def solution(mesh):
    placed = (P("tile", None), P("orient", "tile", None), P(), P("tile"))
    return jax.shard_map(
        functools.partial(per_device, mesh.shape["tile"], mesh.shape["orient"]),
        mesh=mesh,
        in_specs=placed,
        out_specs=(P(("tile", "orient"), None),) * 4,
        check_vma=False,
    )
```

```python
import functools
import math

import jax
import jax.numpy as jnp
import ml_dtypes
import numpy as np
from jax import lax
from jax.experimental import pallas as pl
from jax.experimental.pallas import tpu as pltpu
from jax.sharding import PartitionSpec as P

TS = 512
TPL = 256
MARGIN = TPL // 2
EXT = TS + TPL
HALF = EXT // 2
FREQS = 400
GROUPS = 2
WAVELENGTH = 0.0197
AMPLITUDE = 0.07
ROOT = math.sqrt(3.0) / 2.0
RADIX = 6
SUB = EXT // RADIX
MESH = pl.DeviceIdType.MESH
VMEM = pl.BlockSpec(memory_space=pltpu.VMEM)


def split_table(table):
    high = table.astype(ml_dtypes.bfloat16)
    low = (table - high.astype(np.float64)).astype(ml_dtypes.bfloat16)
    return high, low


@functools.lru_cache(None)
def tables():
    j, n = np.arange(HALF + 1)[:, None], np.arange(EXT)[None, :]
    angle = 2.0 * np.pi * (j * n % EXT) / EXT
    rows = np.zeros((2 * FREQS, EXT))
    rows[: HALF + 1], rows[FREQS : FREQS + HALF + 1] = np.cos(angle), -np.sin(angle)
    own = np.repeat(rows[:, MARGIN : MARGIN + TS].sum(axis=1, keepdims=True), 128, axis=1)
    sample, a = np.arange(SUB)[:, None], np.arange(SUB)[None, :]
    cols = []
    for b in range(RADIX):
        angle = 2.0 * np.pi * (sample * (RADIX * a + b) % EXT) / EXT
        re, im = np.cos(angle), -np.sin(angle)
        cols.append(np.block([[re, im], [-im, re]]))
    p, j = np.arange(TS)[:, None], np.arange(HALF)[None, :]
    angle = 2.0 * np.pi * (p * j % EXT) / EXT
    back_re, back_im = 2.0 * np.cos(angle), -2.0 * np.sin(angle)
    back_re[:, 0] = 1.0
    back_im[:, 0] = (-1.0) ** np.arange(TS)
    back = np.concatenate([back_re, back_im], axis=1)
    cols = np.stack(cols)
    inverse = np.swapaxes(cols, 1, 2)
    return (split_table(rows) + split_table(cols) + (own.astype(np.float32),)
            + split_table(inverse) + split_table(back))


def split(value):
    high = value.astype(jnp.bfloat16)
    return high, (value - high.astype(jnp.float32)).astype(jnp.bfloat16)


def dot3(a, b):
    left = jnp.concatenate([a[0], a[1], a[0]], axis=1)
    right = jnp.concatenate([b[0], b[0], b[1]], axis=0)
    return jnp.dot(left, right, preferred_element_type=jnp.float32)


def turned(x, way):
    re, im = x
    return (way * ROOT) * im - 0.5 * re, (-way * ROOT) * re - 0.5 * im


def plus(x, y):
    return x[0] + y[0], x[1] + y[1]


def minus(x, y):
    return x[0] - y[0], x[1] - y[1]


def three(x, y, z):
    total, apart = plus(y, z), minus(y, z)
    middle = x[0] - 0.5 * total[0], x[1] - 0.5 * total[1]
    side = ROOT * apart[1], -ROOT * apart[0]
    return plus(x, total), plus(middle, side), minus(middle, side)


def circular(turns):
    half = (turns - jnp.round(turns)) * math.pi
    square = half * half
    sine = jnp.full_like(half, 1.0 / math.factorial(13))
    cosine = jnp.full_like(half, -1.0 / math.factorial(14))
    for k in range(5, -1, -1):
        sine = sine * square + (-1.0) ** k / math.factorial(2 * k + 1)
    for k in range(6, -1, -1):
        cosine = cosine * square + (-1.0) ** k / math.factorial(2 * k)
    sine = sine * half
    return 2.0 * sine * cosine, 1.0 - 2.0 * sine * sine


def contrast_vectors(defocus):
    a = lax.broadcasted_iota(jnp.int32, (8, SUB), 1)
    b = lax.broadcasted_iota(jnp.int32, (8, SUB), 0)
    k = RADIX * a + b
    k = jnp.where(k < HALF, k, k - EXT).astype(jnp.float32) * (1.0 / EXT)
    j = jnp.minimum(lax.broadcasted_iota(jnp.int32, (FREQS, 128), 0), HALF)
    j = j.astype(jnp.float32) * (1.0 / EXT)
    rate = (WAVELENGTH / 2.0) * defocus
    sin_k, cos_k = circular(rate * (k * k))
    sin_j, cos_j = circular(rate * (j * j))
    wave = math.sqrt(1.0 - AMPLITUDE * AMPLITUDE)
    factor = -1.0 / (EXT * EXT)
    return (
        (sin_k, cos_k),
        (factor * (wave * cos_j - AMPLITUDE * sin_j), factor * (wave * sin_j + AMPLITUDE * cos_j)),
    )


def body(n, orients, values_ref, group_ref, image_hbm, tmpl_hbm, *rest):
    hbm_tables, rest = rest[:9], rest[9:]
    (out_ref, rows_h, rows_l, cols_h, cols_l, own_sum, inv_h, inv_l, back_h, back_l, image_ref, stats, halo, gath,
     along, down, half_spec, u_h, u_l, wide, v_h, v_l, backs, scores, landed,
     input_sem, table_sem, stat_send, stat_recv, halo_send, halo_recv, far_send, far_recv,
     near_send, near_recv, pass_send, pass_recv, score_send, score_recv) = rest
    me, orient = lax.axis_index("tile"), lax.axis_index("orient")
    lanes, share, shard = orients // GROUPS, TS // orients, TPL // n
    mine, lo = lax.div(orient, lanes), lax.rem(orient, lanes)
    partner = lax.rem(orient + lanes, orients)
    own_shard = pl.ds(pl.multiple_of(me * shard, shard), shard)

    def tile(step):
        return {"tile": lax.rem(me + step, n), "orient": orient}

    def lane(step):
        return {"tile": me, "orient": mine * lanes + lax.rem(lo + step, lanes)}

    across = {"tile": me, "orient": partner}

    def send(src, dst, send_sem, recv_sem, where):
        copy = pltpu.make_async_remote_copy(
            src_ref=src, dst_ref=dst, send_sem=send_sem, recv_sem=recv_sem,
            device_id=where, device_id_type=MESH,
        )
        copy.start()
        return copy

    barrier = pltpu.get_barrier_semaphore()
    for step in range(1, n):
        pl.semaphore_signal(barrier, inc=1, device_id=tile(step), device_id_type=MESH)
    pl.semaphore_signal(barrier, inc=1, device_id=across, device_id_type=MESH)
    for step in range(1, lanes):
        pl.semaphore_signal(barrier, inc=1, device_id=lane(step), device_id_type=MESH)

    held = (rows_h, rows_l, cols_h, cols_l, own_sum, inv_h, inv_l, back_h, back_l)
    loads = [pltpu.make_async_copy(src, dst, table_sem.at[i])
             for i, (src, dst) in enumerate(zip(hbm_tables, held))]
    inputs = [
        pltpu.make_async_copy(image_hbm, image_ref, input_sem.at[0]),
        pltpu.make_async_copy(tmpl_hbm.at[0], gath.at[mine, own_shard], input_sem.at[1]),
    ]
    for load in inputs + loads:
        load.start()
    for load in inputs:
        load.wait()

    image = image_ref[...]
    total = jnp.sum(image)
    squares = jnp.sum(image * image)
    spot = lax.broadcasted_iota(jnp.int32, (8, 128), 1)
    stats[me] = jnp.where(spot == 0, total, jnp.where(spot == 1, squares, 0.0))

    pl.semaphore_wait(barrier, (n - 1) + 1 + (lanes - 1))
    stat_copies = [
        send(stats.at[me], stats.at[me], stat_send.at[s], stat_recv.at[s], tile(s))
        for s in range(1, n)
    ]
    near_copies = [
        send(gath.at[mine, own_shard], gath.at[mine, own_shard], near_send.at[s], near_recv.at[s], tile(s))
        for s in range(1, n)
    ]
    halo_copies = [
        send(image_ref.at[pl.ds(TS - MARGIN, MARGIN)], halo.at[0], halo_send.at[0], halo_recv.at[0], tile(1)),
        send(image_ref.at[pl.ds(0, MARGIN)], halo.at[1], halo_send.at[1], halo_recv.at[1], tile(n - 1)),
    ]
    far_copy = send(gath.at[mine, own_shard], gath.at[mine, own_shard], far_send, far_recv, across)
    wave_along, wave_down = contrast_vectors(values_ref[group_ref[0]])
    for i in range(2):
        along[i] = wave_along[i]

    local = jnp.full((1, TS), total, jnp.float32) * (1.0 / (TS * TS))
    loads[0].wait()
    loads[1].wait()
    inner = slice(MARGIN, MARGIN + TS)
    half_spec[...] = dot3((rows_h[:, inner], rows_l[:, inner]), split(image_ref[...] - local))

    def forward(which):
        tmpl = gath[which]
        centred = tmpl - jnp.sum(tmpl) / (TPL * TPL)
        mean_square = jnp.full((1, TPL), jnp.sum(centred * centred) / (TPL * TPL), jnp.float32)
        normed = centred * (lax.rsqrt(mean_square + 1e-06) * (1.0 / TPL))
        first = dot3((rows_h[:, :TPL], rows_l[:, :TPL]), split(normed))
        near = first[:FREQS, :SUB], first[FREQS:, :SUB]
        far = first[:FREQS, SUB:], first[FREQS:, SUB:]
        once, twice = turned(far, 1), turned(far, -1)
        parts = (plus(near, far), minus(near, twice), plus(near, once),
                 minus(near, far), plus(near, twice), minus(near, once))
        for b, (re, im) in enumerate(parts):
            v_h[b, :, :SUB], v_l[b, :, :SUB] = split(re)
            v_h[b, :, SUB:], v_l[b, :, SUB:] = split(im)

    for copy in near_copies:
        copy.wait()
    forward(mine)

    for copy in stat_copies:
        copy.wait()
    sums = stats[0]
    for step in range(1, n):
        sums = sums + stats[step]
    pixels = float(TS * TS * n)
    centre = jnp.sum(jnp.where(spot == 0, sums, 0.0)) / (8.0 * pixels)
    square = jnp.sum(jnp.where(spot == 1, sums, 0.0)) / (8.0 * pixels)
    centre = jnp.full((1, TS), centre, jnp.float32)
    inverse = lax.rsqrt(square - centre * centre + 1e-05)
    for i in range(2):
        down[i] = wave_down[i] * inverse[:, :128]
    for copy in halo_copies:
        copy.wait()
    before = jnp.where(me > 0, halo[0] - centre, 0.0)
    after = jnp.where(me < n - 1, halo[1] - centre, 0.0)

    far_copy.wait()
    far_shard = gath.at[1 - mine, own_shard]
    pass_copies = [
        send(far_shard, far_shard, pass_send.at[s], pass_recv.at[s], tile(s)) for s in range(1, n)
    ]

    edges = [jnp.concatenate([t[:, :MARGIN], t[:, MARGIN + TS :]], axis=1) for t in (rows_h, rows_l)]
    edge_spec = dot3(edges, split(jnp.concatenate([before, after], axis=0)))
    for load in loads[2:]:
        load.wait()
    shift = own_sum[...] * (local - centre)[:, :128]
    block = []
    for m in range(TS // SUB):
        here = slice(m * SUB, (m + 1) * SUB)
        full = half_spec[:, here] + edge_spec[:, here] + shift
        block.append((full[:FREQS], full[FREQS:]))
    even = three(block[2], plus(block[0], block[3]), block[1])
    flip = (-block[1][0], -block[1][1])
    odd = three(block[2], minus(block[0], block[3]), flip)
    odd = [(-re, -im) for re, im in odd]
    for b, part in enumerate((even[0], odd[2], even[1], odd[0], even[2], odd[1])):
        u_h[b, :, :SUB], u_l[b, :, :SUB] = split(part[0])
        u_h[b, :, SUB:], u_l[b, :, SUB:] = split(part[1])

    for b in range(RADIX):
        spec = dot3((u_h[b], u_l[b]), (cols_h[b], cols_l[b]))
        contrast = along[0, b : b + 1] * down[0] + along[1, b : b + 1] * down[1]
        wide[b, :, :SUB] = spec[:, :SUB] * contrast
        wide[b, :, SUB:] = spec[:, SUB:] * contrast

    score_copies = []
    for turn in range(GROUPS):
        if turn:
            for copy in pass_copies:
                copy.wait()
            forward(1 - mine)
        for b in range(RADIX):
            spec = dot3((v_h[b], v_l[b]), (cols_h[b], cols_l[b]))
            w_re, w_im = wide[b, :, :SUB], wide[b, :, SUB:]
            t_re, t_im = spec[:, :SUB], spec[:, SUB:]
            prod = jnp.concatenate([w_re * t_re + w_im * t_im, w_im * t_re - w_re * t_im], axis=1)
            backs[b] = dot3(split(prod), (inv_h[b], inv_l[b]))

        e = [(backs[b, :, :SUB], backs[b, :, SUB:]) for b in range(RADIX)]
        even = three(e[0], e[2], e[4])
        odd = three(e[3], e[5], e[1])
        outs = plus(even[0], odd[0]), minus(even[2], odd[2]), plus(even[1], odd[1]), minus(even[0], odd[0])
        out_re = jnp.concatenate([re for re, _ in outs], axis=1)
        out_im = jnp.concatenate([im for _, im in outs], axis=1)
        top = lax.broadcasted_iota(jnp.int32, (HALF, 1), 0) == 0
        out_im = jnp.where(top, out_re[HALF : HALF + 1], out_im[:HALF])
        packed = split(jnp.concatenate([out_re[:HALF], out_im], axis=0))
        part = TS // GROUPS
        own = pl.ds(pl.multiple_of(mine * part, part), part)
        scores[turn] = dot3((back_h[own], back_l[own]), packed)
        for step in range(1, lanes):
            start = pl.multiple_of(lax.rem(lo + step, lanes) * share, share)
            score_copies.append(send(
                scores.at[turn, pl.ds(start, share)], landed.at[turn, step],
                score_send.at[turn, step], score_recv.at[turn, step], lane(step),
            ))

    own = pl.ds(pl.multiple_of(lo * share, share), share)
    first, other = scores[0, own], scores[1, own]
    best, second = jnp.maximum(first, other), jnp.minimum(first, other)
    total, squares = first + other, first * first + other * other
    for g in range(GROUPS):
        for step in range(1, lanes):
            score_copies[g * (lanes - 1) + step - 1].wait()
            score = landed[g, step]
            second = jnp.maximum(second, jnp.minimum(best, score))
            best = jnp.maximum(best, score)
            total = total + score
            squares = squares + score * score
    out_ref[0] = best
    out_ref[1] = second
    out_ref[2] = total
    out_ref[3] = squares


def finish(orients, merged_ref, best_ref, second_ref, mean_ref, var_ref):
    best_ref[...] = merged_ref[0]
    second_ref[...] = merged_ref[1]
    mean = merged_ref[2] / orients
    mean_ref[...] = mean
    var_ref[...] = merged_ref[3] / orients - mean * mean


def per_device(n, orients, micrograph, templates, defocus_values, defocus_group):
    f32, b16 = jnp.float32, jnp.bfloat16
    lanes, share = orients // GROUPS, TS // orients
    dma, vmem = pltpu.SemaphoreType.DMA, pltpu.VMEM
    held = [jnp.asarray(t) for t in tables()]
    smem = pl.BlockSpec(memory_space=pltpu.SMEM)
    anywhere = pl.BlockSpec(memory_space=pl.ANY)
    merged = pl.pallas_call(
        functools.partial(body, n, orients),
        out_shape=jax.ShapeDtypeStruct((4, share, TS), f32),
        in_specs=[smem, smem] + [anywhere] * 11,
        out_specs=VMEM,
        scratch_shapes=[vmem(t.shape, t.dtype) for t in held] + [
            vmem((TS, TS), f32),
            vmem((n, 8, 128), f32),
            vmem((2, MARGIN, TS), f32),
            vmem((GROUPS, TPL, TPL), f32),
            vmem((2, 8, SUB), f32),
            vmem((2, FREQS, 128), f32),
            vmem((2 * FREQS, TS), f32),
            vmem((RADIX, FREQS, 2 * SUB), b16),
            vmem((RADIX, FREQS, 2 * SUB), b16),
            vmem((RADIX, FREQS, 2 * SUB), f32),
            vmem((RADIX, FREQS, 2 * SUB), b16),
            vmem((RADIX, FREQS, 2 * SUB), b16),
            vmem((RADIX, FREQS, 2 * SUB), f32),
            vmem((GROUPS, TS // GROUPS, TS), f32),
            vmem((GROUPS, lanes, share, TS), f32),
            dma((2,)), dma((9,)),
            dma((n,)), dma((n,)), dma((2,)), dma((2,)), dma, dma,
            dma((n,)), dma((n,)), dma((n,)), dma((n,)),
            dma((GROUPS, lanes)), dma((GROUPS, lanes)),
        ],
        compiler_params=pltpu.CompilerParams(
            collective_id=0, has_side_effects=True, vmem_limit_bytes=56 * 2**20
        ),
        name="match",
    )(defocus_values, defocus_group, micrograph, templates, *held)
    return pl.pallas_call(
        functools.partial(finish, orients),
        out_shape=(jax.ShapeDtypeStruct((share, TS), f32),) * 4,
        in_specs=[VMEM],
        out_specs=(VMEM,) * 4,
        name="finish",
    )(merged)


def solution(mesh):
    placed = (P("tile", None), P("orient", "tile", None), P(), P("tile"))
    return jax.shard_map(
        functools.partial(per_device, mesh.shape["tile"], mesh.shape["orient"]),
        mesh=mesh,
        in_specs=placed,
        out_specs=(P(("tile", "orient"), None),) * 4,
        check_vma=False,
    )
```

```python
import functools
import math

import jax
import jax.numpy as jnp
import ml_dtypes
import numpy as np
from jax import lax
from jax.experimental import pallas as pl
from jax.experimental.pallas import tpu as pltpu
from jax.sharding import PartitionSpec as P

TS = 512
TPL = 256
MARGIN = TPL // 2
EXT = TS + TPL
HALF = EXT // 2
FREQS = 400
GROUPS = 2
WAVELENGTH = 0.0197
AMPLITUDE = 0.07
ROOT = math.sqrt(3.0) / 2.0
RADIX = 6
SUB = EXT // RADIX
MESH = pl.DeviceIdType.MESH
VMEM = pl.BlockSpec(memory_space=pltpu.VMEM)


def split_table(table):
    high = table.astype(ml_dtypes.bfloat16)
    low = (table - high.astype(np.float64)).astype(ml_dtypes.bfloat16)
    return high, low


@functools.lru_cache(None)
def tables():
    j, n = np.arange(HALF + 1)[:, None], np.arange(EXT)[None, :]
    angle = 2.0 * np.pi * (j * n % EXT) / EXT
    rows = np.zeros((2 * FREQS, EXT))
    rows[: HALF + 1], rows[FREQS : FREQS + HALF + 1] = np.cos(angle), -np.sin(angle)
    own = np.repeat(rows[:, MARGIN : MARGIN + TS].sum(axis=1, keepdims=True), 128, axis=1)
    sample, a = np.arange(SUB)[:, None], np.arange(SUB)[None, :]
    cols = []
    for b in range(RADIX):
        angle = 2.0 * np.pi * (sample * (RADIX * a + b) % EXT) / EXT
        re, im = np.cos(angle), -np.sin(angle)
        cols.append(np.block([[re, im], [-im, re]]))
    p, j = np.arange(TS)[:, None], np.arange(HALF)[None, :]
    angle = 2.0 * np.pi * (p * j % EXT) / EXT
    back_re, back_im = 2.0 * np.cos(angle), -2.0 * np.sin(angle)
    back_re[:, 0] = 1.0
    back_im[:, 0] = (-1.0) ** np.arange(TS)
    back = np.concatenate([back_re, back_im], axis=1)
    return split_table(rows) + split_table(np.stack(cols)) + split_table(back) + (own.astype(np.float32),)


def split(value):
    high = value.astype(jnp.bfloat16)
    return high, (value - high.astype(jnp.float32)).astype(jnp.bfloat16)


def dot(a, b, contract=0):
    return lax.dot_general(
        a, b, (((1,), (contract,)), ((), ())), preferred_element_type=jnp.float32
    )


def dot3(a, b, contract=0):
    left = jnp.concatenate([a[0], a[1], a[0]], axis=1)
    right = jnp.concatenate([b[0], b[0], b[1]], axis=contract)
    return dot(left, right, contract)


def turned(x, way):
    re, im = x
    return (way * ROOT) * im - 0.5 * re, (-way * ROOT) * re - 0.5 * im


def plus(x, y):
    return x[0] + y[0], x[1] + y[1]


def minus(x, y):
    return x[0] - y[0], x[1] - y[1]


def three(x, y, z):
    total, apart = plus(y, z), minus(y, z)
    middle = x[0] - 0.5 * total[0], x[1] - 0.5 * total[1]
    side = ROOT * apart[1], -ROOT * apart[0]
    return plus(x, total), plus(middle, side), minus(middle, side)


def circular(turns):
    half = (turns - jnp.round(turns)) * math.pi
    square = half * half
    sine = jnp.full_like(half, 1.0 / math.factorial(13))
    cosine = jnp.full_like(half, -1.0 / math.factorial(14))
    for k in range(5, -1, -1):
        sine = sine * square + (-1.0) ** k / math.factorial(2 * k + 1)
    for k in range(6, -1, -1):
        cosine = cosine * square + (-1.0) ** k / math.factorial(2 * k)
    sine = sine * half
    return 2.0 * sine * cosine, 1.0 - 2.0 * sine * sine


def contrast_vectors(defocus):
    a = lax.broadcasted_iota(jnp.int32, (8, SUB), 1)
    b = lax.broadcasted_iota(jnp.int32, (8, SUB), 0)
    k = RADIX * a + b
    k = jnp.where(k < HALF, k, k - EXT).astype(jnp.float32) * (1.0 / EXT)
    j = jnp.minimum(lax.broadcasted_iota(jnp.int32, (FREQS, 128), 0), HALF)
    j = j.astype(jnp.float32) * (1.0 / EXT)
    rate = (WAVELENGTH / 2.0) * defocus
    sin_k, cos_k = circular(rate * (k * k))
    sin_j, cos_j = circular(rate * (j * j))
    wave = math.sqrt(1.0 - AMPLITUDE * AMPLITUDE)
    factor = -1.0 / (EXT * EXT)
    return (
        (sin_k, cos_k),
        (factor * (wave * cos_j - AMPLITUDE * sin_j), factor * (wave * sin_j + AMPLITUDE * cos_j)),
    )


def body(n, orients, values_ref, group_ref, image_hbm, tmpl_hbm, *rest):
    hbm_tables, rest = rest[:7], rest[7:]
    (out_ref, rows_h, rows_l, cols_h, cols_l, back_h, back_l, own_sum, image_ref, stats, halo, gath,
     along, down, half_spec, u_h, u_l, wide, v_h, v_l, backs, scores, landed,
     input_sem, table_sem, stat_send, stat_recv, halo_send, halo_recv, far_send, far_recv,
     near_send, near_recv, pass_send, pass_recv, score_send, score_recv) = rest
    me, orient = lax.axis_index("tile"), lax.axis_index("orient")
    lanes, share, shard = orients // GROUPS, TS // orients, TPL // n
    mine, lo = lax.div(orient, lanes), lax.rem(orient, lanes)
    partner = lax.rem(orient + lanes, orients)
    own_shard = pl.ds(pl.multiple_of(me * shard, shard), shard)

    def tile(step):
        return {"tile": lax.rem(me + step, n), "orient": orient}

    def lane(step):
        return {"tile": me, "orient": mine * lanes + lax.rem(lo + step, lanes)}

    across = {"tile": me, "orient": partner}

    def send(src, dst, send_sem, recv_sem, where):
        copy = pltpu.make_async_remote_copy(
            src_ref=src, dst_ref=dst, send_sem=send_sem, recv_sem=recv_sem,
            device_id=where, device_id_type=MESH,
        )
        copy.start()
        return copy

    barrier = pltpu.get_barrier_semaphore()
    for step in range(1, n):
        pl.semaphore_signal(barrier, inc=1, device_id=tile(step), device_id_type=MESH)
    pl.semaphore_signal(barrier, inc=1, device_id=across, device_id_type=MESH)
    for step in range(1, lanes):
        pl.semaphore_signal(barrier, inc=1, device_id=lane(step), device_id_type=MESH)

    held = (rows_h, rows_l, cols_h, cols_l, back_h, back_l, own_sum)
    loads = [pltpu.make_async_copy(src, dst, table_sem.at[i])
             for i, (src, dst) in enumerate(zip(hbm_tables, held))]
    inputs = [
        pltpu.make_async_copy(image_hbm, image_ref, input_sem.at[0]),
        pltpu.make_async_copy(tmpl_hbm.at[0], gath.at[mine, own_shard], input_sem.at[1]),
    ]
    for load in inputs + loads:
        load.start()
    for load in inputs:
        load.wait()

    image = image_ref[...]
    total = jnp.sum(image)
    squares = jnp.sum(image * image)
    spot = lax.broadcasted_iota(jnp.int32, (8, 128), 1)
    stats[me] = jnp.where(spot == 0, total, jnp.where(spot == 1, squares, 0.0))

    pl.semaphore_wait(barrier, (n - 1) + 1 + (lanes - 1))
    stat_copies = [
        send(stats.at[me], stats.at[me], stat_send.at[s], stat_recv.at[s], tile(s))
        for s in range(1, n)
    ]
    halo_copies = [
        send(image_ref.at[pl.ds(TS - MARGIN, MARGIN)], halo.at[0], halo_send.at[0], halo_recv.at[0], tile(1)),
        send(image_ref.at[pl.ds(0, MARGIN)], halo.at[1], halo_send.at[1], halo_recv.at[1], tile(n - 1)),
    ]
    far_copy = send(gath.at[mine, own_shard], gath.at[mine, own_shard], far_send, far_recv, across)
    near_copies = [
        send(gath.at[mine, own_shard], gath.at[mine, own_shard], near_send.at[s], near_recv.at[s], tile(s))
        for s in range(1, n)
    ]

    wave_along, wave_down = contrast_vectors(values_ref[group_ref[0]])
    for i in range(2):
        along[i] = wave_along[i]

    local = jnp.full((1, TS), total, jnp.float32) * (1.0 / (TS * TS))
    loads[0].wait()
    loads[1].wait()
    inner = slice(MARGIN, MARGIN + TS)
    half_spec[...] = dot3((rows_h[:, inner], rows_l[:, inner]), split(image_ref[...] - local))

    for copy in stat_copies:
        copy.wait()
    sums = stats[0]
    for step in range(1, n):
        sums = sums + stats[step]
    pixels = float(TS * TS * n)
    centre = jnp.sum(jnp.where(spot == 0, sums, 0.0)) / (8.0 * pixels)
    square = jnp.sum(jnp.where(spot == 1, sums, 0.0)) / (8.0 * pixels)
    centre = jnp.full((1, TS), centre, jnp.float32)
    inverse = lax.rsqrt(square - centre * centre + 1e-05)
    for i in range(2):
        down[i] = wave_down[i] * inverse[:, :128]
    for copy in halo_copies:
        copy.wait()
    before = jnp.where(me > 0, halo[0] - centre, 0.0)
    after = jnp.where(me < n - 1, halo[1] - centre, 0.0)

    far_copy.wait()
    far_shard = gath.at[1 - mine, own_shard]
    pass_copies = [
        send(far_shard, far_shard, pass_send.at[s], pass_recv.at[s], tile(s)) for s in range(1, n)
    ]

    edges = [jnp.concatenate([t[:, :MARGIN], t[:, MARGIN + TS :]], axis=1) for t in (rows_h, rows_l)]
    edge_spec = dot3(edges, split(jnp.concatenate([before, after], axis=0)))
    for load in loads[2:]:
        load.wait()
    shift = own_sum[...] * (local - centre)[:, :128]
    block = []
    for m in range(TS // SUB):
        here = slice(m * SUB, (m + 1) * SUB)
        full = half_spec[:, here] + edge_spec[:, here] + shift
        block.append((full[:FREQS], full[FREQS:]))
    even = three(block[2], plus(block[0], block[3]), block[1])
    flip = (-block[1][0], -block[1][1])
    odd = three(block[2], minus(block[0], block[3]), flip)
    odd = [(-re, -im) for re, im in odd]
    for b, part in enumerate((even[0], odd[2], even[1], odd[0], even[2], odd[1])):
        u_h[b, :, :SUB], u_l[b, :, :SUB] = split(part[0])
        u_h[b, :, SUB:], u_l[b, :, SUB:] = split(part[1])

    def forward(which):
        tmpl = gath[which]
        centred = tmpl - jnp.sum(tmpl) / (TPL * TPL)
        mean_square = jnp.full((1, TPL), jnp.sum(centred * centred) / (TPL * TPL), jnp.float32)
        normed = centred * (lax.rsqrt(mean_square + 1e-06) * (1.0 / TPL))
        first = dot3((rows_h[:, :TPL], rows_l[:, :TPL]), split(normed))
        near = first[:FREQS, :SUB], first[FREQS:, :SUB]
        far = first[:FREQS, SUB:], first[FREQS:, SUB:]
        once, twice = turned(far, 1), turned(far, -1)
        parts = (plus(near, far), minus(near, twice), plus(near, once),
                 minus(near, far), plus(near, twice), minus(near, once))
        for b, (re, im) in enumerate(parts):
            v_h[b, :, :SUB], v_l[b, :, :SUB] = split(re)
            v_h[b, :, SUB:], v_l[b, :, SUB:] = split(im)

    for copy in near_copies:
        copy.wait()
    forward(mine)
    for b in range(RADIX):
        spec = dot3((u_h[b], u_l[b]), (cols_h[b], cols_l[b]))
        contrast = along[0, b : b + 1] * down[0] + along[1, b : b + 1] * down[1]
        wide[b, :, :SUB] = spec[:, :SUB] * contrast
        wide[b, :, SUB:] = spec[:, SUB:] * contrast

    score_copies = []
    for turn in range(GROUPS):
        if turn:
            for copy in pass_copies:
                copy.wait()
            forward(1 - mine)
        for b in range(RADIX):
            spec = dot3((v_h[b], v_l[b]), (cols_h[b], cols_l[b]))
            w_re, w_im = wide[b, :, :SUB], wide[b, :, SUB:]
            t_re, t_im = spec[:, :SUB], spec[:, SUB:]
            prod = jnp.concatenate([w_re * t_re + w_im * t_im, w_im * t_re - w_re * t_im], axis=1)
            backs[b] = dot3(split(prod), (cols_h[b], cols_l[b]), 1)

        e = [(backs[b, :, :SUB], backs[b, :, SUB:]) for b in range(RADIX)]
        even = three(e[0], e[2], e[4])
        odd = three(e[3], e[5], e[1])
        outs = plus(even[0], odd[0]), minus(even[2], odd[2]), plus(even[1], odd[1]), minus(even[0], odd[0])
        out_re = jnp.concatenate([re for re, _ in outs], axis=1)
        out_im = jnp.concatenate([im for _, im in outs], axis=1)
        top = lax.broadcasted_iota(jnp.int32, (HALF, 1), 0) == 0
        out_im = jnp.where(top, out_re[HALF : HALF + 1], out_im[:HALF])
        packed = split(jnp.concatenate([out_re[:HALF], out_im], axis=0))
        part = TS // GROUPS
        own = pl.ds(pl.multiple_of(mine * part, part), part)
        scores[turn] = dot3((back_h[own], back_l[own]), packed)
        for step in range(1, lanes):
            start = pl.multiple_of(lax.rem(lo + step, lanes) * share, share)
            score_copies.append(send(
                scores.at[turn, pl.ds(start, share)], landed.at[turn, step],
                score_send.at[turn, step], score_recv.at[turn, step], lane(step),
            ))

    own = pl.ds(pl.multiple_of(lo * share, share), share)
    first, other = scores[0, own], scores[1, own]
    best, second = jnp.maximum(first, other), jnp.minimum(first, other)
    total, squares = first + other, first * first + other * other
    for g in range(GROUPS):
        for step in range(1, lanes):
            score_copies[g * (lanes - 1) + step - 1].wait()
            score = landed[g, step]
            second = jnp.maximum(second, jnp.minimum(best, score))
            best = jnp.maximum(best, score)
            total = total + score
            squares = squares + score * score
    out_ref[0] = best
    out_ref[1] = second
    mean = total / orients
    out_ref[2] = mean
    out_ref[3] = squares / orients - mean * mean


def finish(merged_ref, *rest):
    outs, sems = rest[:4], rest[4]
    copies = [pltpu.make_async_copy(merged_ref.at[i], out, sems.at[i]) for i, out in enumerate(outs)]
    for copy in copies:
        copy.start()
    for copy in copies:
        copy.wait()


def per_device(n, orients, micrograph, templates, defocus_values, defocus_group):
    f32, b16 = jnp.float32, jnp.bfloat16
    lanes, share = orients // GROUPS, TS // orients
    dma, vmem = pltpu.SemaphoreType.DMA, pltpu.VMEM
    held = [jnp.asarray(t) for t in tables()]
    smem = pl.BlockSpec(memory_space=pltpu.SMEM)
    anywhere = pl.BlockSpec(memory_space=pl.ANY)
    merged = pl.pallas_call(
        functools.partial(body, n, orients),
        out_shape=jax.ShapeDtypeStruct((4, share, TS), f32),
        in_specs=[smem, smem] + [anywhere] * 9,
        out_specs=VMEM,
        scratch_shapes=[vmem(t.shape, t.dtype) for t in held] + [
            vmem((TS, TS), f32),
            vmem((n, 8, 128), f32),
            vmem((2, MARGIN, TS), f32),
            vmem((GROUPS, TPL, TPL), f32),
            vmem((2, 8, SUB), f32),
            vmem((2, FREQS, 128), f32),
            vmem((2 * FREQS, TS), f32),
            vmem((RADIX, FREQS, 2 * SUB), b16),
            vmem((RADIX, FREQS, 2 * SUB), b16),
            vmem((RADIX, FREQS, 2 * SUB), f32),
            vmem((RADIX, FREQS, 2 * SUB), b16),
            vmem((RADIX, FREQS, 2 * SUB), b16),
            vmem((RADIX, FREQS, 2 * SUB), f32),
            vmem((GROUPS, TS // GROUPS, TS), f32),
            vmem((GROUPS, lanes, share, TS), f32),
            dma((2,)), dma((7,)),
            dma((n,)), dma((n,)), dma((2,)), dma((2,)), dma, dma,
            dma((n,)), dma((n,)), dma((n,)), dma((n,)),
            dma((GROUPS, lanes)), dma((GROUPS, lanes)),
        ],
        compiler_params=pltpu.CompilerParams(
            collective_id=0, has_side_effects=True, vmem_limit_bytes=56 * 2**20
        ),
        name="match",
    )(defocus_values, defocus_group, micrograph, templates, *held)
    return pl.pallas_call(
        finish,
        out_shape=(jax.ShapeDtypeStruct((share, TS), f32),) * 4,
        in_specs=[anywhere],
        out_specs=(anywhere,) * 4,
        scratch_shapes=[dma((4,))],
        name="finish",
    )(merged)


def solution(mesh):
    placed = (P("tile", None), P("orient", "tile", None), P(), P("tile"))
    return jax.shard_map(
        functools.partial(per_device, mesh.shape["tile"], mesh.shape["orient"]),
        mesh=mesh,
        in_specs=placed,
        out_specs=(P(("tile", "orient"), None),) * 4,
        check_vma=False,
    )
```

```python
import functools
import math

import jax
import jax.numpy as jnp
import ml_dtypes
import numpy as np
from jax import lax
from jax.experimental import pallas as pl
from jax.experimental.pallas import tpu as pltpu
from jax.sharding import PartitionSpec as P

TS = 512
TPL = 256
MARGIN = TPL // 2
EXT = TS + TPL
HALF = EXT // 2
FREQS = 400
GROUPS = 2
WAVELENGTH = 0.0197
AMPLITUDE = 0.07
ROOT = math.sqrt(3.0) / 2.0
RADIX = 6
SUB = EXT // RADIX
MESH = pl.DeviceIdType.MESH
VMEM = pl.BlockSpec(memory_space=pltpu.VMEM)


def split_table(table):
    high = table.astype(ml_dtypes.bfloat16)
    low = (table - high.astype(np.float64)).astype(ml_dtypes.bfloat16)
    return high, low


@functools.lru_cache(None)
def tables():
    j, n = np.arange(HALF + 1)[:, None], np.arange(EXT)[None, :]
    angle = 2.0 * np.pi * (j * n % EXT) / EXT
    rows = np.zeros((2 * FREQS, EXT))
    rows[: HALF + 1], rows[FREQS : FREQS + HALF + 1] = np.cos(angle), -np.sin(angle)
    own = np.stack([
        np.repeat(rows[:, part].sum(axis=1, keepdims=True), 128, axis=1)
        for part in (slice(MARGIN, MARGIN + TS), slice(0, MARGIN), slice(MARGIN + TS, EXT))
    ])
    sample, a = np.arange(SUB)[:, None], np.arange(SUB)[None, :]
    cols = []
    for b in range(RADIX):
        angle = 2.0 * np.pi * (sample * (RADIX * a + b) % EXT) / EXT
        re, im = np.cos(angle), -np.sin(angle)
        cols.append(np.block([[re, im], [-im, re]]))
    p, j = np.arange(TS)[:, None], np.arange(HALF)[None, :]
    angle = 2.0 * np.pi * (p * j % EXT) / EXT
    back_re, back_im = 2.0 * np.cos(angle), -2.0 * np.sin(angle)
    back_re[:, 0] = 1.0
    back_im[:, 0] = (-1.0) ** np.arange(TS)
    back = np.concatenate([back_re, back_im], axis=1)
    return split_table(rows) + split_table(np.stack(cols)) + split_table(back) + (own.astype(np.float32),)


def split(value):
    high = value.astype(jnp.bfloat16)
    return high, (value - high.astype(jnp.float32)).astype(jnp.bfloat16)


def dot(a, b, contract=0):
    return lax.dot_general(
        a, b, (((1,), (contract,)), ((), ())), preferred_element_type=jnp.float32
    )


def dot3(a, b, contract=0):
    left = jnp.concatenate([a[0], a[1], a[0]], axis=1)
    right = jnp.concatenate([b[0], b[0], b[1]], axis=contract)
    return dot(left, right, contract)


def turned(x, way):
    re, im = x
    return (way * ROOT) * im - 0.5 * re, (-way * ROOT) * re - 0.5 * im


def plus(x, y):
    return x[0] + y[0], x[1] + y[1]


def minus(x, y):
    return x[0] - y[0], x[1] - y[1]


def three(x, y, z):
    total, apart = plus(y, z), minus(y, z)
    middle = x[0] - 0.5 * total[0], x[1] - 0.5 * total[1]
    side = ROOT * apart[1], -ROOT * apart[0]
    return plus(x, total), plus(middle, side), minus(middle, side)


def circular(turns):
    half = (turns - jnp.round(turns)) * math.pi
    square = half * half
    sine = jnp.full_like(half, 1.0 / math.factorial(13))
    cosine = jnp.full_like(half, -1.0 / math.factorial(14))
    for k in range(5, -1, -1):
        sine = sine * square + (-1.0) ** k / math.factorial(2 * k + 1)
    for k in range(6, -1, -1):
        cosine = cosine * square + (-1.0) ** k / math.factorial(2 * k)
    sine = sine * half
    return 2.0 * sine * cosine, 1.0 - 2.0 * sine * sine


def contrast_vectors(defocus):
    a = lax.broadcasted_iota(jnp.int32, (8, SUB), 1)
    b = lax.broadcasted_iota(jnp.int32, (8, SUB), 0)
    k = RADIX * a + b
    k = jnp.where(k < HALF, k, k - EXT).astype(jnp.float32) * (1.0 / EXT)
    j = jnp.minimum(lax.broadcasted_iota(jnp.int32, (FREQS, 128), 0), HALF)
    j = j.astype(jnp.float32) * (1.0 / EXT)
    rate = (WAVELENGTH / 2.0) * defocus
    sin_k, cos_k = circular(rate * (k * k))
    sin_j, cos_j = circular(rate * (j * j))
    wave = math.sqrt(1.0 - AMPLITUDE * AMPLITUDE)
    factor = -1.0 / (EXT * EXT)
    return (
        (sin_k, cos_k),
        (factor * (wave * cos_j - AMPLITUDE * sin_j), factor * (wave * sin_j + AMPLITUDE * cos_j)),
    )


def body(n, orients, values_ref, group_ref, image_hbm, tmpl_hbm, *rest):
    hbm_tables, rest = rest[:7], rest[7:]
    (out_ref, rows_h, rows_l, cols_h, cols_l, back_h, back_l, own_sum, image_ref, stats, halo, gath,
     along, down, half_spec, u_h, u_l, wide, v_h, v_l, backs, scores, landed,
     input_sem, table_sem, stat_send, stat_recv, halo_send, halo_recv, far_send, far_recv,
     near_send, near_recv, pass_send, pass_recv, score_send, score_recv) = rest
    me, orient = lax.axis_index("tile"), lax.axis_index("orient")
    lanes, share, shard = orients // GROUPS, TS // orients, TPL // n
    mine, lo = lax.div(orient, lanes), lax.rem(orient, lanes)
    partner = lax.rem(orient + lanes, orients)
    own_shard = pl.ds(pl.multiple_of(me * shard, shard), shard)

    def tile(step):
        return {"tile": lax.rem(me + step, n), "orient": orient}

    def lane(step):
        return {"tile": me, "orient": mine * lanes + lax.rem(lo + step, lanes)}

    across = {"tile": me, "orient": partner}

    def send(src, dst, send_sem, recv_sem, where):
        copy = pltpu.make_async_remote_copy(
            src_ref=src, dst_ref=dst, send_sem=send_sem, recv_sem=recv_sem,
            device_id=where, device_id_type=MESH,
        )
        copy.start()
        return copy

    barrier = pltpu.get_barrier_semaphore()
    for step in range(1, n):
        pl.semaphore_signal(barrier, inc=1, device_id=tile(step), device_id_type=MESH)
    pl.semaphore_signal(barrier, inc=1, device_id=across, device_id_type=MESH)
    for step in range(1, lanes):
        pl.semaphore_signal(barrier, inc=1, device_id=lane(step), device_id_type=MESH)

    held = (rows_h, rows_l, cols_h, cols_l, back_h, back_l, own_sum)
    loads = [pltpu.make_async_copy(src, dst, table_sem.at[i])
             for i, (src, dst) in enumerate(zip(hbm_tables, held))]
    inputs = [
        pltpu.make_async_copy(image_hbm, image_ref, input_sem.at[0]),
        pltpu.make_async_copy(tmpl_hbm.at[0], gath.at[mine, own_shard], input_sem.at[1]),
    ]
    for load in inputs + loads:
        load.start()
    pl.semaphore_wait(barrier, (n - 1) + 1 + (lanes - 1))
    halo_copies = [
        send(image_hbm.at[pl.ds(TS - MARGIN, MARGIN)], halo.at[0], halo_send.at[0], halo_recv.at[0], tile(1)),
        send(image_hbm.at[pl.ds(0, MARGIN)], halo.at[1], halo_send.at[1], halo_recv.at[1], tile(n - 1)),
    ]
    for load in inputs:
        load.wait()

    image = image_ref[...]
    total = jnp.sum(image)
    squares = jnp.sum(image * image)
    spot = lax.broadcasted_iota(jnp.int32, (8, 128), 1)
    stats[me] = jnp.where(spot == 0, total, jnp.where(spot == 1, squares, 0.0))
    stat_copies = [
        send(stats.at[me], stats.at[me], stat_send.at[s], stat_recv.at[s], tile(s))
        for s in range(1, n)
    ]
    far_copy = send(tmpl_hbm.at[0], gath.at[mine, own_shard], far_send, far_recv, across)
    near_copies = [
        send(tmpl_hbm.at[0], gath.at[mine, own_shard], near_send.at[s], near_recv.at[s], tile(s))
        for s in range(1, n)
    ]

    wave_along, wave_down = contrast_vectors(values_ref[group_ref[0]])
    for i in range(2):
        along[i] = wave_along[i]

    local = jnp.full((1, TS), total, jnp.float32) * (1.0 / (TS * TS))
    loads[0].wait()
    loads[1].wait()
    inner = slice(MARGIN, MARGIN + TS)
    half_spec[...] = dot3((rows_h[:, inner], rows_l[:, inner]), split(image_ref[...] - local))

    for copy in halo_copies:
        copy.wait()
    before = jnp.where(me > 0, halo[0] - local, 0.0)
    after = jnp.where(me < n - 1, halo[1] - local, 0.0)

    edges = [jnp.concatenate([t[:, :MARGIN], t[:, MARGIN + TS :]], axis=1) for t in (rows_h, rows_l)]
    edge_spec = dot3(edges, split(jnp.concatenate([before, after], axis=0)))
    for copy in stat_copies:
        copy.wait()
    sums = stats[0]
    for step in range(1, n):
        sums = sums + stats[step]
    pixels = float(TS * TS * n)
    centre = jnp.sum(jnp.where(spot == 0, sums, 0.0)) / (8.0 * pixels)
    square = jnp.sum(jnp.where(spot == 1, sums, 0.0)) / (8.0 * pixels)
    centre = jnp.full((1, TS), centre, jnp.float32)
    inverse = lax.rsqrt(square - centre * centre + 1e-05)
    for i in range(2):
        down[i] = wave_down[i] * inverse[:, :128]
    for load in loads[2:]:
        load.wait()
    present = own_sum[0] + jnp.where(me > 0, own_sum[1], 0.0)
    present = present + jnp.where(me < n - 1, own_sum[2], 0.0)
    shift = present * (local - centre)[:, :128]
    block = []
    for m in range(TS // SUB):
        here = slice(m * SUB, (m + 1) * SUB)
        full = half_spec[:, here] + edge_spec[:, here] + shift
        block.append((full[:FREQS], full[FREQS:]))
    even = three(block[2], plus(block[0], block[3]), block[1])
    flip = (-block[1][0], -block[1][1])
    odd = three(block[2], minus(block[0], block[3]), flip)
    odd = [(-re, -im) for re, im in odd]
    for b, part in enumerate((even[0], odd[2], even[1], odd[0], even[2], odd[1])):
        u_h[b, :, :SUB], u_l[b, :, :SUB] = split(part[0])
        u_h[b, :, SUB:], u_l[b, :, SUB:] = split(part[1])

    def forward(which):
        tmpl = gath[which]
        centred = tmpl - jnp.sum(tmpl) / (TPL * TPL)
        mean_square = jnp.full((1, TPL), jnp.sum(centred * centred) / (TPL * TPL), jnp.float32)
        normed = centred * (lax.rsqrt(mean_square + 1e-06) * (1.0 / TPL))
        first = dot3((rows_h[:, :TPL], rows_l[:, :TPL]), split(normed))
        near = first[:FREQS, :SUB], first[FREQS:, :SUB]
        far = first[:FREQS, SUB:], first[FREQS:, SUB:]
        once, twice = turned(far, 1), turned(far, -1)
        parts = (plus(near, far), minus(near, twice), plus(near, once),
                 minus(near, far), plus(near, twice), minus(near, once))
        for b, (re, im) in enumerate(parts):
            v_h[b, :, :SUB], v_l[b, :, :SUB] = split(re)
            v_h[b, :, SUB:], v_l[b, :, SUB:] = split(im)

    far_copy.wait()
    far_shard = gath.at[1 - mine, own_shard]
    pass_copies = [
        send(far_shard, far_shard, pass_send.at[s], pass_recv.at[s], tile(s)) for s in range(1, n)
    ]
    for b in range(RADIX):
        spec = dot3((u_h[b], u_l[b]), (cols_h[b], cols_l[b]))
        contrast = along[0, b : b + 1] * down[0] + along[1, b : b + 1] * down[1]
        wide[b, :, :SUB] = spec[:, :SUB] * contrast
        wide[b, :, SUB:] = spec[:, SUB:] * contrast

    score_copies = []
    for turn in range(GROUPS):
        for copy in pass_copies if turn else near_copies:
            copy.wait()
        forward(1 - mine if turn else mine)
        for b in range(RADIX):
            spec = dot3((v_h[b], v_l[b]), (cols_h[b], cols_l[b]))
            w_re, w_im = wide[b, :, :SUB], wide[b, :, SUB:]
            t_re, t_im = spec[:, :SUB], spec[:, SUB:]
            prod = jnp.concatenate([w_re * t_re + w_im * t_im, w_im * t_re - w_re * t_im], axis=1)
            backs[b] = dot3(split(prod), (cols_h[b], cols_l[b]), 1)

        e = [(backs[b, :, :SUB], backs[b, :, SUB:]) for b in range(RADIX)]
        even = three(e[0], e[2], e[4])
        odd = three(e[3], e[5], e[1])
        outs = plus(even[0], odd[0]), minus(even[2], odd[2]), plus(even[1], odd[1]), minus(even[0], odd[0])
        out_re = jnp.concatenate([re for re, _ in outs], axis=1)
        out_im = jnp.concatenate([im for _, im in outs], axis=1)
        top = lax.broadcasted_iota(jnp.int32, (HALF, 1), 0) == 0
        out_im = jnp.where(top, out_re[HALF : HALF + 1], out_im[:HALF])
        packed = split(jnp.concatenate([out_re[:HALF], out_im], axis=0))
        part = TS // GROUPS
        own = pl.ds(pl.multiple_of(mine * part, part), part)
        scores[turn] = dot3((back_h[own], back_l[own]), packed)
        for step in range(1, lanes):
            start = pl.multiple_of(lax.rem(lo + step, lanes) * share, share)
            score_copies.append(send(
                scores.at[turn, pl.ds(start, share)], landed.at[turn, step],
                score_send.at[turn, step], score_recv.at[turn, step], lane(step),
            ))

    own = pl.ds(pl.multiple_of(lo * share, share), share)
    first, other = scores[0, own], scores[1, own]
    best, second = jnp.maximum(first, other), jnp.minimum(first, other)
    total, squares = first + other, first * first + other * other
    for g in range(GROUPS):
        for step in range(1, lanes):
            score_copies[g * (lanes - 1) + step - 1].wait()
            score = landed[g, step]
            second = jnp.maximum(second, jnp.minimum(best, score))
            best = jnp.maximum(best, score)
            total = total + score
            squares = squares + score * score
    out_ref[0] = best
    out_ref[1] = second
    mean = total / orients
    out_ref[2] = mean
    out_ref[3] = squares / orients - mean * mean


def finish(merged_ref, *outs):
    for i, out in enumerate(outs):
        out[...] = merged_ref[i]


def per_device(n, orients, micrograph, templates, defocus_values, defocus_group):
    f32, b16 = jnp.float32, jnp.bfloat16
    lanes, share = orients // GROUPS, TS // orients
    dma, vmem = pltpu.SemaphoreType.DMA, pltpu.VMEM
    held = [jnp.asarray(t) for t in tables()]
    smem = pl.BlockSpec(memory_space=pltpu.SMEM)
    anywhere = pl.BlockSpec(memory_space=pl.ANY)
    merged = pl.pallas_call(
        functools.partial(body, n, orients),
        out_shape=jax.ShapeDtypeStruct((4, share, TS), f32),
        in_specs=[smem, smem] + [anywhere] * 9,
        out_specs=VMEM,
        scratch_shapes=[vmem(t.shape, t.dtype) for t in held] + [
            vmem((TS, TS), f32),
            vmem((n, 8, 128), f32),
            vmem((2, MARGIN, TS), f32),
            vmem((GROUPS, TPL, TPL), f32),
            vmem((2, 8, SUB), f32),
            vmem((2, FREQS, 128), f32),
            vmem((2 * FREQS, TS), f32),
            vmem((RADIX, FREQS, 2 * SUB), b16),
            vmem((RADIX, FREQS, 2 * SUB), b16),
            vmem((RADIX, FREQS, 2 * SUB), f32),
            vmem((RADIX, FREQS, 2 * SUB), b16),
            vmem((RADIX, FREQS, 2 * SUB), b16),
            vmem((RADIX, FREQS, 2 * SUB), f32),
            vmem((GROUPS, TS // GROUPS, TS), f32),
            vmem((GROUPS, lanes, share, TS), f32),
            dma((2,)), dma((7,)),
            dma((n,)), dma((n,)), dma((2,)), dma((2,)), dma, dma,
            dma((n,)), dma((n,)), dma((n,)), dma((n,)),
            dma((GROUPS, lanes)), dma((GROUPS, lanes)),
        ],
        compiler_params=pltpu.CompilerParams(
            collective_id=0, has_side_effects=True, vmem_limit_bytes=56 * 2**20
        ),
        name="match",
    )(defocus_values, defocus_group, micrograph, templates, *held)
    return pl.pallas_call(
        finish,
        out_shape=(jax.ShapeDtypeStruct((share, TS), f32),) * 4,
        in_specs=[VMEM],
        out_specs=(VMEM,) * 4,
        name="finish",
    )(merged)


def solution(mesh):
    placed = (P("tile", None), P("orient", "tile", None), P(), P("tile"))
    return jax.shard_map(
        functools.partial(per_device, mesh.shape["tile"], mesh.shape["orient"]),
        mesh=mesh,
        in_specs=placed,
        out_specs=(P(("tile", "orient"), None),) * 4,
        check_vma=False,
    )
```
